32 devices in a mesh: dp: 2 (over x), expert: 16 (over z, y, core).
Axes of the slice: x: 2, y: 2, z: 4, core: 2. Of those that a mesh axis runs over, the one named last changes fastest.
Arguments:
- latent: bfloat16 [4096, 1024], P(('dp', 'expert')), may hold values from -6 to 6
- routes: int32 [4096, 8], P(('dp', 'expert')), may hold values from 0 to 15, all different within a row; in each aligned block of 128 rows (0 to 127, 128 to 255, ...) at most 80 rows name the same one
- gates: float32 [4096, 8], P(('dp', 'expert')), may hold values from 0.05 to 0.5
- grad_out: bfloat16 [4096, 4096], P(('dp', 'expert')), may hold values from -6 to 6
- w_out_t: bfloat16 [4096, 1024], P('expert'), may hold values from -0.1875 to 0.1875
- expert_up: bfloat16 [16, 1024, 2048], P('expert'), may hold values from -0.1875 to 0.1875
- expert_down: bfloat16 [16, 2048, 1024], P('expert'), may hold values from -0.125 to 0.125
Outputs:
- mixed: bfloat16 [4096, 4096], P(('dp', 'expert'))
- grad_latent: bfloat16 [4096, 1024], P(('dp', 'expert'))
- grad_w_out: float32 [4096, 1024], P('expert')
The draws below stay inside these ranges and needn't reach their ends.
Inputs may be any that keep to these rules, and one draw needn't show every extreme that they name: `routes`: within the 128 rows of one device each row names 8 different experts, and no expert is named by more than 80 of those rows; some expert is named by exactly 80 rows of some device.
All inputs are finite; a program needn't handle non-finite values.
Results may differ from the reference program's by a relative error of at most 0.02.
Values may be sent and summed in bfloat16 or wider, within the bound.
No kernel may reach another device: no remote copies, remote signals or barrier semaphores. Data moves between devices by JAX's collectives and lax.ppermute only.
A program may use at most 128 MiB of HBM per device.

```python
import math
import jax
import jax.numpy as jnp
import numpy as np
from jax import lax

D = 4096
L = 1024
H = 2048
K = 8
TOK_DEV = 128
EXPERTS = 16
TOKENS = 4096
CAP = 80
N_DP = 2
N_EXPERT = 16


def block_levels(stream_key, shape, shards, least, high):
    loudness = 1.0
    for dim, blocks in shards:
        heights = jax.random.uniform(jax.random.fold_in(jax.random.fold_in(stream_key, 6), dim), (blocks,), jnp.float32, least / len(shards), high / len(shards))
        loudness = loudness * jnp.repeat(jnp.exp(heights), shape[dim] // blocks).reshape((-1,) + (1,) * (len(shape) - 1 - dim))
    return loudness


def assign_block(key, own, number, rows, number_of, top, limit, slope):
    ranking = jax.random.permutation(key, number_of)
    heavy_load, usual = load_shares(number_of, rows * top, limit, slope, True), load_shares(number_of, rows * top, limit, slope, False)
    places = jnp.arange(number_of)

    def named(tallies, turn):
        used = int((tallies > 0).sum())
        fixed = max(1, used // 4)
        shifted = fixed + (places - fixed + turn * (used - fixed)) % max(1, number_of - fixed)
        return jnp.zeros((number_of,), jnp.int32).at[ranking[jnp.where(places < fixed, places, shifted)]].set(jnp.asarray(tallies, jnp.int32))

    tallies = jnp.where(number % 4 == 0, named(heavy_load, number // 4), named(usual, number - number // 4 - 1))
    mixed = jax.random.permutation(jax.random.fold_in(own, 3), number_of)
    donor, receiver = mixed[0:number_of // 2 * 2:2], mixed[1:number_of // 2 * 2:2]
    margin = jnp.minimum(tallies[donor] - 1, limit - tallies[receiver]) // 2
    margin = jnp.where((donor == ranking[0]) | (receiver == ranking[0]) | (tallies[receiver] == 0), 0, jnp.maximum(margin, 0))
    shifted = jax.random.randint(jax.random.fold_in(own, 4), (number_of // 2,), 0, 1 << 20) % (margin + 1)
    tallies = tallies.at[donor].add(-shifted).at[receiver].add(shifted)
    labels = jnp.searchsorted(jnp.cumsum(tallies), jnp.arange(rows * top), side="right").astype(jnp.int32)
    table = labels.reshape(top, rows).T
    table = table[jax.random.permutation(jax.random.fold_in(own, 1), rows)]
    turn = jax.random.randint(jax.random.fold_in(own, 2), (rows, 1), 0, top)
    return jnp.take_along_axis(table, (jnp.arange(top)[None, :] + turn) % top, axis=1)


def load_shares(amount, total, most, skew, full):
    weights = [(1 << 20) // math.isqrt(rank ** skew) + 1 for rank in range(1, amount + 1)]
    largest = most if full else min(most, max(-(-total // amount), total * weights[0] // sum(weights)))
    least = 1 if total - largest >= amount - 1 else 0
    counts, rest = [largest] + [least] * (amount - 1), total - largest - least * (amount - 1)
    while rest > 0:
        candidates = [i for i in range(1, amount) if counts[i] < largest] or [i for i in range(1, amount) if counts[i] < most]
        pool, left = sum([weights[i] for i in candidates]), rest
        for i in candidates:
            extra = min(most - counts[i], max(1, left * weights[i] // pool), rest)
            counts[i] = counts[i] + extra
            rest = rest - extra
    return np.array(counts)


def normal_values(stream_key, dims, scale, limit, cuts=(), held_as=jnp.bfloat16):
    level = block_levels(stream_key, dims, cuts, -0.22, 0.18) if cuts else 1.0
    drawn = jax.random.normal(stream_key, dims, jnp.float32) * scale * level
    return jnp.minimum(jnp.maximum(drawn, -limit), limit).astype(held_as)


def setup_inputs(seed: int = 0) -> dict:
    key_list = jax.random.split(jax.random.key(seed), 8)
    latent = normal_values(key_list[0], (TOKENS, L), 1.0, 6.0, ((0, 32),))
    routes_keys = jax.random.split(jax.random.fold_in(key_list[1], 1), TOKENS // TOK_DEV)
    routes_turns = jax.random.permutation(jax.random.fold_in(key_list[1], 3), TOKENS // TOK_DEV)
    routes = jax.vmap(lambda own, number: assign_block(jax.random.fold_in(key_list[1], 2), own, number, TOK_DEV, EXPERTS, K, CAP, 1))(routes_keys, routes_turns).reshape((TOKENS, K))
    gates = jnp.clip(0.05 + 0.45 * jax.random.uniform(key_list[2], (TOKENS, K), jnp.float32) ** block_levels(key_list[2], (TOKENS, K), ((0, 32),), -0.2, 0.2), 0.05, 0.5)
    grad_out = normal_values(key_list[3], (TOKENS, D), 1.0, 6.0, ((0, 32),))
    w_out_t = normal_values(key_list[4], (D, L), L ** -0.5, 0.1875, ((0, 16),))
    expert_up = normal_values(key_list[5], (EXPERTS, L, H), L ** -0.5, 0.1875, ((0, 16),))
    expert_down = normal_values(key_list[6], (EXPERTS, H, L), H ** -0.5, 0.125, ((0, 16),))
    return {"latent": latent, "routes": routes, "gates": gates, "grad_out": grad_out, "w_out_t": w_out_t, "expert_up": expert_up, "expert_down": expert_down}


def expert_forward(rows, up_weight, down_weight):
    pre = jnp.dot(rows.astype(jnp.float32), up_weight.astype(jnp.float32), preferred_element_type=jnp.float32)
    act = (jnp.maximum(pre, 0.0) ** 2).astype(jnp.bfloat16)
    return jnp.dot(act.astype(jnp.float32), down_weight.astype(jnp.float32), preferred_element_type=jnp.float32).astype(jnp.bfloat16)


def expert_backward(rows, grads, up_weight, down_weight):
    pre = jnp.dot(rows.astype(jnp.float32), up_weight.astype(jnp.float32), preferred_element_type=jnp.float32)
    grad_act = jnp.dot(grads.astype(jnp.float32), down_weight.astype(jnp.float32).T, preferred_element_type=jnp.float32)
    grad_pre = (grad_act * 2.0 * jnp.maximum(pre, 0.0)).astype(jnp.bfloat16)
    return jnp.dot(grad_pre.astype(jnp.float32), up_weight.astype(jnp.float32).T, preferred_element_type=jnp.float32).astype(jnp.bfloat16)


def reference(latent, routes, gates, grad_out, w_out_t, expert_up, expert_down):
    blocks = N_DP * N_EXPERT
    width = latent.shape[1]
    flat = routes.reshape(blocks, TOK_DEV * K)
    onehot = (flat[:, :, None] == jnp.arange(EXPERTS, dtype=jnp.int32)[None, None, :]).astype(jnp.int32)
    before = jnp.cumsum(onehot, axis=1) - onehot
    slots = jnp.sum(before * onehot, axis=2).astype(jnp.int32)
    owner = jnp.arange(blocks, dtype=jnp.int32)[:, None]
    target = ((flat * blocks + owner) * CAP + slots).reshape(-1).astype(jnp.int32)
    repeated = jnp.repeat(latent, K, axis=0)
    buffer = jnp.zeros((EXPERTS * blocks * CAP, width), jnp.bfloat16).at[target].set(repeated)
    buffer = buffer.reshape(EXPERTS, blocks * CAP, width)
    outputs = lax.map(lambda item: expert_forward(item[0], item[1], item[2]), (buffer, expert_up, expert_down))
    picked = outputs.reshape(-1, width)[target].astype(jnp.float32).reshape(TOKENS, K, width)
    combined = jnp.sum(picked * gates[:, :, None], axis=1).astype(jnp.bfloat16)
    mixed = jnp.dot(combined, w_out_t.T, preferred_element_type=jnp.float32).astype(jnp.bfloat16)
    grad_combined = jnp.dot(grad_out, w_out_t, preferred_element_type=jnp.float32).astype(jnp.bfloat16)
    grad_w_out = jnp.dot(grad_out.T, combined, preferred_element_type=jnp.float32)
    scaled = (jnp.repeat(grad_combined, K, axis=0).astype(jnp.float32) * gates.reshape(-1, 1)).astype(jnp.bfloat16)
    grad_buffer = jnp.zeros((EXPERTS * blocks * CAP, width), jnp.bfloat16).at[target].set(scaled)
    grad_buffer = grad_buffer.reshape(EXPERTS, blocks * CAP, width)
    grad_rows = lax.map(lambda item: expert_backward(item[0], item[1], item[2], item[3]), (buffer, grad_buffer, expert_up, expert_down))
    gathered = grad_rows.reshape(-1, width)[target].astype(jnp.float32).reshape(TOKENS, K, width)
    grad_latent = jnp.sum(gathered, axis=1).astype(jnp.bfloat16)
    return mixed, grad_latent, grad_w_out
```

```python
import functools

import jax
import jax.numpy as jnp
from jax import lax
from jax.experimental import pallas as pl
from jax.experimental.pallas import tpu as pltpu
from jax.sharding import PartitionSpec as P

BF16 = jnp.bfloat16
F32 = jnp.float32
LANES = 128
NN = (((1,), (0,)), ((), ()))
NT = (((1,), (1,)), ((), ()))
TN = (((0,), (0,)), ((), ()))


def dot(a, b, dims=NN):
    return lax.dot_general(a, b, dims, preferred_element_type=F32)


def cost(flops, moved):
    return pl.CostEstimate(flops=int(flops), bytes_accessed=int(moved), transcendentals=0)


def whole(shape):
    return pl.BlockSpec(shape, lambda *_: (0,) * len(shape))


SMEM = pl.BlockSpec(memory_space=pltpu.SMEM)
ANY = pl.BlockSpec(memory_space=pl.ANY)
VMEM_BYTES = 60 * 1024 * 1024


def ring_order(chips):
    return list(range(0, chips, 2)) + list(range(1, chips, 2))[::-1]


def shift(x, chips, step):
    order = ring_order(chips)
    pairs = [
        (2 * order[j] + core, 2 * order[(j + step) % chips] + core)
        for j in range(chips)
        for core in range(2)
    ]
    return lax.ppermute(x, "expert", pairs)


def swap(x, chips):
    return lax.ppermute(x, "expert", [(i, i ^ 1) for i in range(2 * chips)])


def together(*values):
    flat, tree = jax.tree.flatten(values)
    return jax.tree.unflatten(tree, lax.optimization_barrier(flat))


class View:
    def __init__(self, x, low=0, count=None):
        self.x, self.low = x, low
        self.count = x.shape[0] - low if count is None else count

    def rows(self, start, stop):
        return View(self.x, self.low + start, stop - start)

    def value(self):
        return self.x[self.low : self.low + self.count]


def cut(views, start, stop):
    found, base = [], 0
    for v in views:
        low, high = max(start, base), min(stop, base + v.count)
        if low < high:
            found.append(v.rows(low - base, high - base))
        base += v.count
    return found


def join(views):
    values = [v.value() for v in views]
    return values[0] if len(values) == 1 else jnp.concatenate(values, axis=0)


def move_group(blocks, how):
    moved, base, found = how(join([v for b in blocks for v in b])), 0, []
    for b in blocks:
        count = sum(v.count for v in b)
        found.append([View(moved, base, count)])
        base += count
    return found


def ring_step(chips, rings, beside=()):
    sent = [r.send() for r in rings]
    up, down = join([u for u, _ in sent]), join([d for _, d in sent])
    up, down, beside = together(shift(up, chips, 1), shift(down, chips, -1), beside)
    u_base = d_base = 0
    for ring, (u, d) in zip(rings, sent):
        ring.receive(View(up, u_base, u.count), View(down, d_base, d.count))
        u_base, d_base = u_base + u.count, d_base + d.count
    return beside


class Gather:
    def __init__(self, x, chips, cut_row):
        self.half, self.steps, self.cut_row = chips // 2, 0, cut_row
        self.got, self.wire = {0: [View(x)]}, (View(x), View(x))

    def send(self):
        self.steps += 1
        up, down = self.wire
        if self.steps < self.half:
            return up, down
        return up.rows(0, self.cut_row), down.rows(self.cut_row, down.count)

    def receive(self, up, down):
        self.wire = up, down
        if self.steps < self.half:
            self.got[-self.steps], self.got[self.steps] = [up], [down]
        else:
            self.got[self.steps] = [up, down]


def total(terms):
    return functools.reduce(jnp.add, [t.astype(F32) for t in terms])


class Scatter:
    def __init__(self, parts, chips):
        self.half, self.left, self.parts, self.wire = chips // 2, chips // 2, parts, None

    def send(self):
        s, self.left = self.left, self.left - 1
        if s == self.half:
            far = total(self.parts[s]).astype(BF16)
            self.cut_row = far.shape[0] // 2
            up, down = far[: self.cut_row], far[self.cut_row :]
        else:
            (up, down), at = self.wire, self.cut_row
            a, b = total(self.parts[s]), total(self.parts[-s])
            if s == self.half - 1:
                up = jnp.concatenate([a[:at] + up.astype(F32), a[at:]], axis=0)
                down = jnp.concatenate([b[:at], b[at:] + down.astype(F32)], axis=0)
            else:
                up, down = a + up.astype(F32), b + down.astype(F32)
        return View(up.astype(BF16)), View(down.astype(BF16))

    def receive(self, up, down):
        self.wire = up.value(), down.value()

    def sum(self):
        return total(list(self.parts[0]) + list(self.wire))


def local_call(kernel, name, scalars, arrays, outs, scratch, flops, moved):
    return pl.pallas_call(
        kernel,
        in_specs=[SMEM] * len(scalars) + [ANY] * len(arrays),
        out_specs=[ANY] * len(outs),
        out_shape=outs,
        scratch_shapes=scratch,
        compiler_params=pltpu.CompilerParams(vmem_limit_bytes=VMEM_BYTES),
        cost_estimate=cost(flops, moved),
        name=name,
    )(*scalars, *arrays)


class Pieces:
    def __init__(self):
        self.arrays, self.items = [], []

    def add(self, views, slot, to=0):
        for v in views:
            known = [k for k, x in enumerate(self.arrays) if x is v.x]
            if not known:
                self.arrays.append(v.x)
                known = [len(self.arrays) - 1]
            self.items.append((known[0], v.low, v.count, slot, to))
            to += v.count

    def copies(self, refs, buffer, sems, first):
        by_slot = {}
        for i, (k, low, size, slot, to) in enumerate(self.items):
            dst = buffer.at[slot, pl.ds(to, size)]
            src = refs[k].at[pl.ds(low, size), pl.ds(0, buffer.shape[2])]
            copy = pltpu.make_async_copy(src, dst, sems.at[first + i])
            by_slot.setdefault(slot, []).append(copy)
        return by_slot


def start(copies):
    for c in copies:
        c.start()


def wait(copies):
    for c in copies:
        c.wait()


def pair_gates(gate, pair, cap, tokens):
    first = gate[2 * pair * cap : (2 * pair + 1) * cap, :]
    second = gate[(2 * pair + 1) * cap : (2 * pair + 2) * cap, :]
    empty = jnp.zeros((cap, tokens), F32)
    return jnp.concatenate(
        [jnp.concatenate([first, empty], 1), jnp.concatenate([empty, second], 1)], 0
    )


def picks(gate):
    return jnp.where(gate > 0.0, 1.0, 0.0).astype(BF16)


def tile_of(i, tile):
    return pl.ds(pl.multiple_of(i * tile, tile), tile)


def weight_copies(hbm, vmem, sems, first, tile, i):
    here, count = tile_of(i, tile), hbm[0].shape[1] // tile
    return [
        pltpu.make_async_copy(hbm[0].at[:, here], vmem[0].at[:, here], sems.at[first + i]),
        pltpu.make_async_copy(hbm[1].at[here, :], vmem[1].at[here, :], sems.at[first + count + i]),
    ]


def part_copies(both, pair, tokens, part_refs, swap_ref, sems, first):
    return [
        pltpu.make_async_copy(both.at[pair, pl.ds(0, tokens)], part_refs[pair], sems.at[first + 2 * pair]),
        pltpu.make_async_copy(
            both.at[pair, pl.ds(tokens, tokens)],
            swap_ref.at[pl.ds(pair * tokens, tokens)],
            sems.at[first + 2 * pair + 1],
        ),
    ]


def forward_kernel(pairs, cap, tokens, tile, toks, exts, me_ref, *refs):
    n_tok, n_ext = len(toks.arrays), len(exts.arrays)
    tok_refs, ext_refs = refs[:n_tok], refs[n_tok : n_tok + n_ext]
    refs = refs[n_tok + n_ext :]
    n_tok, n_ext = len(toks.items), len(exts.items)
    weights_hbm, (relu_hbm, gate_hbm) = refs[:2], refs[2:4]
    part_refs, swap_ref = refs[4 : 4 + pairs], refs[4 + pairs]
    both, ext, up, down, relu, gate, rows, acc, masks, in_sem, out_sem = refs[5 + pairs :]
    count, tiles = 2 * pairs, up.shape[1] // tile

    ext_in = exts.copies(ext_refs, ext, in_sem, 0)
    tok_in = toks.copies(tok_refs, both, in_sem, n_ext)
    for copies in (*ext_in.values(), *tok_in.values()):
        start(copies)
    first = n_ext + n_tok
    for i in range(tiles):
        start(weight_copies(weights_hbm, (up, down), in_sem, first, tile, i))

    masks[...] = jnp.zeros_like(masks)
    for b in range(count):
        wait(ext_in[b])
        extra = ext[b].astype(F32)
        mine = lax.broadcasted_iota(jnp.int32, extra.shape, 0) == me_ref[0]
        line = jnp.sum(jnp.where(mine, extra, 0.0), axis=0, keepdims=True)
        masks[b : b + 1, :] = (
            line[:, :tokens] + line[:, tokens : 2 * tokens]
        ) + line[:, 2 * tokens : 3 * tokens]
    earlier = (
        lax.broadcasted_iota(jnp.int32, (tokens, tokens), 0)
        < lax.broadcasted_iota(jnp.int32, (tokens, tokens), 1)
    )
    chosen = picks(masks[...])
    slots = dot(chosen, jnp.where(earlier, 1.0, 0.0).astype(BF16)).astype(jnp.int32)
    place = lax.broadcasted_iota(jnp.int32, (cap, tokens), 0)
    for b in range(count):
        gate[b * cap : (b + 1) * cap, :] = jnp.where(
            place == slots[b : b + 1, :], masks[b : b + 1, :], 0.0
        )
    gate_out = pltpu.make_async_copy(gate, gate_hbm, out_sem.at[0])
    gate_out.start()
    for p in range(pairs):
        wait(tok_in[p])
        pick = picks(pair_gates(gate, p, cap, tokens))
        rows[2 * p * cap : (2 * p + 2) * cap, :] = dot(pick, both[p]).astype(BF16)

    def relu_copy(i):
        here = tile_of(i, tile)
        return pltpu.make_async_copy(relu.at[:, here], relu_hbm.at[:, here], out_sem.at[1 + i])

    def hidden_tile(i, begin):
        here = tile_of(i, tile)
        wait(weight_copies(weights_hbm, (up, down), in_sem, first, tile, i))
        pre = jnp.maximum(dot(rows[...], up[:, here]), 0.0)
        relu[:, here] = pre.astype(BF16)
        relu_copy(i).start()
        out = dot((pre * pre).astype(BF16), down[here, :])
        acc[...] = out if begin else acc[...] + out

    hidden_tile(0, True)
    pl.loop(1, tiles)(lambda i: hidden_tile(i, False))

    parts_out = []
    for p in range(pairs):
        scale = pair_gates(gate, p, cap, tokens)
        result = acc[2 * p * cap : (2 * p + 2) * cap, :].astype(BF16).astype(F32)
        scaled = (result * jnp.sum(scale, axis=1, keepdims=True)).astype(BF16)
        both[p] = dot(picks(scale), scaled, TN).astype(BF16)
        out = part_copies(both, p, tokens, part_refs, swap_ref, out_sem, 1 + tiles)
        start(out)
        parts_out += out
    wait(parts_out + [gate_out] + [relu_copy(i) for i in range(tiles)])


def backward_kernel(pairs, cap, tokens, tile, toks, *refs):
    tok_refs, refs = refs[: len(toks.arrays)], refs[len(toks.arrays) :]
    relu_hbm, gate_hbm, weights_hbm = refs[0], refs[1], refs[2:4]
    part_refs, swap_ref = refs[4 : 4 + pairs], refs[4 + pairs]
    both, up, down, relu, gate, rows, acc, in_sem, out_sem = refs[5 + pairs :]
    tiles = up.shape[1] // tile

    gate_in = pltpu.make_async_copy(gate_hbm, gate, in_sem.at[0])
    gate_in.start()
    tok_in = toks.copies(tok_refs, both, in_sem, 1)
    for copies in tok_in.values():
        start(copies)
    first = 1 + len(toks.items)

    def tile_copies(i):
        here = tile_of(i, tile)
        copy = pltpu.make_async_copy(relu_hbm.at[:, here], relu.at[:, here], in_sem.at[first + i])
        return weight_copies(weights_hbm, (up, down), in_sem, first + tiles, tile, i) + [copy]

    for i in range(tiles):
        start(tile_copies(i))

    gate_in.wait()
    for p in range(pairs):
        wait(tok_in[p])
        scale = pair_gates(gate, p, cap, tokens)
        rows[2 * p * cap : (2 * p + 2) * cap, :] = (
            dot(picks(scale), both[p]) * jnp.sum(scale, axis=1, keepdims=True)
        ).astype(BF16)

    def hidden_tile(i, begin):
        here = tile_of(i, tile)
        wait(tile_copies(i))
        grad_act = dot(rows[...], down[here, :], NT)
        grad_pre = (grad_act * 2.0 * relu[:, here].astype(F32)).astype(BF16)
        out = dot(grad_pre, up[:, here], NT)
        acc[...] = out if begin else acc[...] + out

    hidden_tile(0, True)
    pl.loop(1, tiles)(lambda i: hidden_tile(i, False))

    parts_out = []
    for p in range(pairs):
        pick = picks(pair_gates(gate, p, cap, tokens))
        grad_rows = acc[2 * p * cap : (2 * p + 2) * cap, :].astype(BF16)
        both[p] = dot(pick, grad_rows, TN).astype(BF16)
        out = part_copies(both, p, tokens, part_refs, swap_ref, out_sem, 0)
        start(out)
        parts_out += out
    wait(parts_out)


def part_shapes(pairs, tokens, width):
    shapes = [jax.ShapeDtypeStruct((tokens, width), BF16)] * pairs
    return shapes + [jax.ShapeDtypeStruct((pairs * tokens, width), BF16)]


def expert_forward(me, blocks, extra, up, down, cap, tokens):
    pairs, (width, hidden) = len(blocks) // 2, up.shape
    count, tile = len(blocks), min(512, hidden)
    toks, exts = Pieces(), Pieces()
    for b, block in enumerate(blocks):
        toks.add(cut(block, 0, tokens), b // 2, b % 2 * tokens)
        exts.add(cut(block, tokens, tokens + extra), b)
    outs = [
        jax.ShapeDtypeStruct((count * cap, hidden), BF16),
        jax.ShapeDtypeStruct((count * cap, tokens), F32),
    ] + part_shapes(pairs, tokens, width)
    scratch = [
        pltpu.VMEM((pairs, 2 * tokens, width), BF16),
        pltpu.VMEM((count, extra, 3 * tokens), BF16),
        pltpu.VMEM((width, hidden), BF16),
        pltpu.VMEM((hidden, width), BF16),
        pltpu.VMEM((count * cap, hidden), BF16),
        pltpu.VMEM((count * cap, tokens), F32),
        pltpu.VMEM((count * cap, width), BF16),
        pltpu.VMEM((count * cap, width), F32),
        pltpu.VMEM((-(-count // 16) * 16, tokens), F32),
        pltpu.SemaphoreType.DMA((len(toks.items) + len(exts.items) + 2 * (hidden // tile),)),
        pltpu.SemaphoreType.DMA((1 + hidden // tile + count,)),
    ]
    out = local_call(
        functools.partial(forward_kernel, pairs, cap, tokens, tile, toks, exts),
        "expert_forward", [me], [*toks.arrays, *exts.arrays, up, down], outs, scratch,
        4 * count * cap * width * hidden, 4 * width * hidden,
    )
    return out[0], out[1], list(out[2:-1]), out[-1]


def expert_backward(blocks, relu, gate, up, down, cap, tokens):
    pairs, (width, hidden) = len(blocks) // 2, up.shape
    count, tile = len(blocks), min(512, hidden)
    toks = Pieces()
    for b, block in enumerate(blocks):
        toks.add(block, b // 2, b % 2 * tokens)
    scratch = [
        pltpu.VMEM((pairs, 2 * tokens, width), BF16),
        pltpu.VMEM((width, hidden), BF16),
        pltpu.VMEM((hidden, width), BF16),
        pltpu.VMEM((count * cap, hidden), BF16),
        pltpu.VMEM((count * cap, tokens), F32),
        pltpu.VMEM((count * cap, width), BF16),
        pltpu.VMEM((count * cap, width), F32),
        pltpu.SemaphoreType.DMA((1 + len(toks.items) + 3 * (hidden // tile),)),
        pltpu.SemaphoreType.DMA((count,)),
    ]
    out = local_call(
        functools.partial(backward_kernel, pairs, cap, tokens, tile, toks),
        "expert_backward", [], [*toks.arrays, relu, gate, up, down],
        part_shapes(pairs, tokens, width), scratch,
        4 * count * cap * width * hidden, 4 * width * hidden,
    )
    return list(out[:-1]), out[-1]


def columns(offsets, k, rows):
    return pl.ds(pl.multiple_of(offsets[k] * rows, rows), rows)


def narrow_columns(x, cols, rows):
    return x.reshape(x.shape[0], -1, rows)[:, cols, :].reshape(x.shape[0], -1)


def shard_columns(grads, offsets, k, count, rows):
    return jnp.concatenate(
        [grads[0, :, columns(offsets, k, rows)], grads[0, :, columns(offsets, count + k, rows)]], 1
    )


def stacked(mine, other):
    return jnp.concatenate([join(b) for b in (*mine, *other)], axis=0)


def projection_pieces(mine, other, rows):
    pieces = Pieces()
    for k in range(len(mine)):
        pieces.add(mine[k], k, 0)
        pieces.add(other[k], k, rows)
    return pieces


def both_cores(pair, rows):
    pieces = Pieces()
    pieces.add([View(pair[0])], 0, 0)
    pieces.add([View(pair[1])], 0, rows)
    return pieces


def grad_combined_kernel(rows, acts, weights, offsets, *refs):
    n_act, n_weight = len(acts.arrays), len(weights.arrays)
    act_refs, weight_refs = refs[:n_act], refs[n_act : n_act + n_weight]
    own_ref, sib_ref, grads, weight, out, in_sem, out_sem = refs[n_act + n_weight :]
    tokens, count = own_ref.shape[0], weight.shape[0]
    act_in = acts.copies(act_refs, grads, in_sem, 0)[0]
    weight_in = weights.copies(weight_refs, weight, in_sem, len(acts.items))
    start(act_in)
    for k in range(count):
        start(weight_in[k])
    wait(act_in)
    total = jnp.zeros(out.shape, F32)
    for k in range(count):
        wait(weight_in[k])
        total += dot(shard_columns(grads, offsets, k, count, rows), weight[k])
    out[...] = total
    copies = [
        pltpu.make_async_copy(out.at[pl.ds(0, tokens)], own_ref, out_sem.at[0]),
        pltpu.make_async_copy(out.at[pl.ds(tokens, tokens)], sib_ref, out_sem.at[1]),
    ]
    start(copies)
    wait(copies)


def grad_combined_part(offsets, grads, mine, other, rows, width):
    (tokens, features), count = grads[0].shape, len(mine)
    if rows % LANES:
        weight = stacked(mine, other)
        return [dot(narrow_columns(g, offsets, rows), weight) for g in grads]
    acts, weights = both_cores(grads, tokens), projection_pieces(mine, other, rows)
    return local_call(
        functools.partial(grad_combined_kernel, rows, acts, weights),
        "grad_combined", [offsets], [*acts.arrays, *weights.arrays],
        [jax.ShapeDtypeStruct((tokens, width), F32)] * 2,
        [
            pltpu.VMEM((1, 2 * tokens, features), BF16),
            pltpu.VMEM((count, 2 * rows, width), BF16),
            pltpu.VMEM((2 * tokens, width), F32),
            pltpu.SemaphoreType.DMA((len(acts.items) + len(weights.items),)),
            pltpu.SemaphoreType.DMA((2,)),
        ],
        8 * tokens * rows * count * width, 4 * rows * count * width,
    )


def mixed_kernel(rows, acts, weights, *refs):
    n_act, n_weight = len(acts.arrays), len(weights.arrays)
    act_refs, weight_refs = refs[:n_act], refs[n_act : n_act + n_weight]
    own_ref, sib_ref, comb, weight, out, in_sem, out_sem = refs[n_act + n_weight :]
    tokens, count = own_ref.shape[0], weight.shape[0]
    act_in = acts.copies(act_refs, comb, in_sem, 0)[0]
    weight_in = weights.copies(weight_refs, weight, in_sem, len(acts.items))
    start(act_in)
    for k in range(count):
        start(weight_in[k])
    wait(act_in)
    for k in range(count):
        wait(weight_in[k])
        block = dot(comb[0], weight[k], NT).astype(BF16)
        for part in range(2):
            here = slice((part * count + k) * rows, (part * count + k + 1) * rows)
            out[:, here] = block[:, part * rows : (part + 1) * rows]
    copies = [
        pltpu.make_async_copy(out.at[pl.ds(0, tokens)], own_ref, out_sem.at[0]),
        pltpu.make_async_copy(out.at[pl.ds(tokens, tokens)], sib_ref, out_sem.at[1]),
    ]
    start(copies)
    wait(copies)


def mixed_part(combs, mine, other, rows):
    (tokens, width), count = combs[0].shape, len(mine)
    if rows % LANES:
        weight = stacked(mine, other)
        return [dot(c, weight, NT).astype(BF16) for c in combs]
    acts, weights = both_cores(combs, tokens), projection_pieces(mine, other, rows)
    return local_call(
        functools.partial(mixed_kernel, rows, acts, weights),
        "mixed", [], [*acts.arrays, *weights.arrays],
        [jax.ShapeDtypeStruct((tokens, 2 * count * rows), BF16)] * 2,
        [
            pltpu.VMEM((1, 2 * tokens, width), BF16),
            pltpu.VMEM((count, 2 * rows, width), BF16),
            pltpu.VMEM((2 * tokens, 2 * count * rows), BF16),
            pltpu.SemaphoreType.DMA((len(acts.items) + len(weights.items),)),
            pltpu.SemaphoreType.DMA((2,)),
        ],
        8 * tokens * rows * count * width, 4 * rows * count * width,
    )


def place_kernel(count, rows, offsets, own_ref, other_ref, out_ref):
    for k in range(count):
        block = slice(k * rows, (k + 1) * rows)
        out_ref[:, columns(offsets, k, rows)] = own_ref[:, block]
        out_ref[:, columns(offsets, count + k, rows)] = other_ref[:, block]


def place_columns(offsets, own, other, rows):
    count = offsets.shape[0] // 2
    if rows % LANES:
        back = jnp.zeros_like(offsets).at[offsets].set(jnp.arange(2 * count, dtype=offsets.dtype))
        return narrow_columns(jnp.concatenate([own, other], axis=1), back, rows)
    out = jax.ShapeDtypeStruct((own.shape[0], 2 * own.shape[1]), BF16)
    return pl.pallas_call(
        functools.partial(place_kernel, count, rows),
        in_specs=[SMEM, whole(own.shape), whole(other.shape)],
        out_specs=whole(out.shape),
        out_shape=out,
        grid=(1,),
        compiler_params=pltpu.CompilerParams(vmem_limit_bytes=VMEM_BYTES),
        cost_estimate=cost(0, 8 * own.size),
        name="place_columns",
    )(offsets, own, other)


def weight_grad_kernel(grads, combs, core_ref, *refs):
    n_grad, n_comb = len(grads.arrays), len(combs.arrays)
    grad_refs, comb_refs = refs[:n_grad], refs[n_grad : n_grad + n_comb]
    own_ref, sib_ref, grad, comb, out, rounded, in_sem, out_sem = refs[n_grad + n_comb :]
    rows = own_ref.shape[0]
    copies = grads.copies(grad_refs, grad, in_sem, 0)[0]
    copies += combs.copies(comb_refs, comb, in_sem, len(grads.items))[0]
    start(copies)
    wait(copies)
    out[...] = dot(grad[0], comb[0], TN)
    rounded[...] = out[...].astype(BF16)
    own = pl.ds(pl.multiple_of(core_ref[0] * rows, rows), rows)
    sib = pl.ds(pl.multiple_of((1 - core_ref[0]) * rows, rows), rows)
    copies = [
        pltpu.make_async_copy(out.at[own], own_ref, out_sem.at[0]),
        pltpu.make_async_copy(rounded.at[sib], sib_ref, out_sem.at[1]),
    ]
    start(copies)
    wait(copies)


def weight_grad(core, grads, combs):
    (tokens, features), width = grads[0].shape, combs[0][0].x.shape[1]
    grad, comb = Pieces(), Pieces()
    for k, (g, c) in enumerate(zip(grads, combs)):
        grad.add([View(g)], 0, k * tokens)
        comb.add(c, 0, k * tokens)
    count, rows = len(grads), features // 2
    return local_call(
        functools.partial(weight_grad_kernel, grad, comb),
        "weight_grad", [core], [*grad.arrays, *comb.arrays],
        [jax.ShapeDtypeStruct((rows, width), F32), jax.ShapeDtypeStruct((rows, width), BF16)],
        [
            pltpu.VMEM((1, count * tokens, features), BF16),
            pltpu.VMEM((1, count * tokens, width), BF16),
            pltpu.VMEM((features, width), F32),
            pltpu.VMEM((features, width), BF16),
            pltpu.SemaphoreType.DMA((len(grad.items) + len(comb.items),)),
            pltpu.SemaphoreType.DMA((2,)),
        ],
        2 * count * tokens * features * width, 2 * count * tokens * (features + width),
    )


def gate_rows(routes, gates, experts, width):
    chosen = routes.T[None] == jnp.arange(experts, dtype=jnp.int32)[:, None, None]
    gate = jnp.sum(jnp.where(chosen, gates.T[None], 0.0), axis=1)
    high = lax.reduce_precision(gate, 8, 7)
    middle = lax.reduce_precision(gate - high, 8, 7)
    low = gate - high - middle
    terms = jnp.concatenate([high, middle, low], axis=1).astype(BF16)
    return jnp.pad(terms, ((0, 0), (0, width - terms.shape[1])))


def on_device(latent, routes, gates, grad_out, w_out_t, expert_up, expert_down):
    tokens, width = latent.shape
    members = lax.axis_size("expert")
    chips = members // 2
    half = chips // 2
    capacity = max(4, tokens * routes.shape[1] * 5 // (4 * members))
    cap = -(-capacity // 16) * 16
    up_weight, down_weight = expert_up[0], expert_down[0]

    me = lax.axis_index("expert").astype(jnp.int32)
    chip, core = me // 2, me % 2
    position = jnp.where(chip % 2 == 0, chip // 2, chips - 1 - chip // 2)
    dists = [0] + [d for s in range(1, half) for d in (-s, s)] + [half]
    there = (position + jnp.array(dists, jnp.int32)) % chips
    chip_there = jnp.where(there < half, 2 * there, 2 * (chips - 1 - there) + 1)
    own_cols, sib_cols = 2 * chip_there + core, 2 * chip_there + 1 - core
    me, core = me.reshape(1), core.reshape(1)
    groups = [[0, -1, 1]] + [[-s, s] for s in range(2, half)] + [[half]]

    dp, replica = lax.axis_size("dp"), lax.axis_index("dp").astype(jnp.int32)
    shard = w_out_t.shape[0]
    piece = shard // dp
    own_parts = jnp.concatenate([own_cols * 2 + replica, own_cols * 2 + 1 - replica])
    sib_parts = jnp.concatenate([sib_cols * 2 + replica, sib_cols * 2 + 1 - replica])

    def partner(x):
        return lax.ppermute(x, "dp", [(i, (i + 1) % dp) for i in range(dp)])

    def half_rows(which):
        return lax.dynamic_slice_in_dim(w_out_t, which * piece, piece, 0)

    def core_swap(gathered, group, size):
        own = [cut(gathered.got[d], 0, size) for d in group]
        other = move_group(own, lambda x: swap(x, chips))
        return [side for pair in zip(own, other) for side in pair]

    def share_out(group, parts, other, into):
        swapped = swap(other, chips)
        for i, d in enumerate(group):
            into[d] = [parts[i], swapped[i * tokens : (i + 1) * tokens]]

    extra = members
    begin, end = tokens + extra, tokens + extra + piece
    block = jnp.concatenate(
        [latent, gate_rows(routes, gates, members, width), half_rows(replica)], axis=0
    )
    ring = Gather(block, chips, tokens)
    other_half = {0: half_rows(1 - replica)}
    forward, backward, kept = {}, {}, []

    def run_forward(i):
        pairs = core_swap(ring, groups[i], tokens + extra)
        return expert_forward(me, pairs, extra, up_weight, down_weight, cap, tokens)

    def keep_forward(i, out):
        kept.append(out[:2])
        share_out(groups[i], *out[2:], forward)

    def exchange(ds):
        return partner(join([v for d in ds for v in cut(ring.got[d], begin, end)]))

    def keep_half(ds, got):
        for i, d in enumerate(ds):
            other_half[d] = got[i * piece : (i + 1) * piece]

    grads = (grad_out, ring_step(chips, [ring], swap(grad_out, chips)))
    for s in range(2, half + 1):
        ds = [1 - s, s - 1]
        out, got = ring_step(chips, [ring], (run_forward(s - 2), exchange(ds)))
        keep_forward(s - 2, out)
        keep_half(ds, got)

    def column_block(d):
        chip_at = chip_there[dists.index(d)]
        return lax.dynamic_slice_in_dim(grad_out, chip_at * 2 * shard, 2 * shard, 1)

    def send_columns(ds):
        return [shift(column_block(half if d == half else -d), chips, -d) for d in ds]

    ordered = dists[:0:-1]
    first, second = len(ordered) * 3 // 7, len(ordered) * 5 // 7
    col_blocks = {0: column_block(0)}

    out, got, cols = together(
        run_forward(half - 1), exchange([half]), send_columns(ordered[:first])
    )
    keep_forward(half - 1, out)
    keep_half([half], got)
    col_blocks.update(zip(ordered[:first], cols))

    mine = [cut(ring.got[d], begin, end) for d in dists]
    others = [[View(other_half[d])] for d in dists]
    comb = Scatter(forward, chips)
    gc_own, gc_swap = grad_combined_part(own_parts, grads, mine, others, piece, width)
    gc_other, cols = ring_step(
        chips, [comb], (swap(gc_swap, chips), send_columns(ordered[first:second]))
    )
    col_blocks.update(zip(ordered[first:second], cols))
    grad_ring = Gather((gc_own + gc_other).astype(BF16), chips, tokens // 2)

    def run_backward(i):
        pairs = core_swap(grad_ring, groups[i], tokens)
        return expert_backward(pairs, *kept[i], up_weight, down_weight, cap, tokens)

    ring_step(chips, [comb, grad_ring])
    for s in range(2, half):
        out = ring_step(chips, [comb, grad_ring], run_backward(s - 2))
        share_out(groups[s - 2], *out, backward)
    combined = comb.sum().astype(BF16)
    comb_ring = Gather(combined, chips, tokens // 2)
    out = ring_step(chips, [grad_ring, comb_ring], run_backward(half - 2))
    share_out(groups[half - 2], *out, backward)
    out, cols, comb_other = ring_step(
        chips,
        [comb_ring],
        (run_backward(half - 1), send_columns(ordered[second:]), swap(combined, chips)),
    )
    share_out(groups[half - 1], *out, backward)
    col_blocks.update(zip(ordered[second:], cols))

    back = Scatter(backward, chips)
    mixed = mixed_part((combined, comb_other), mine, others, piece)
    mixed = ring_step(chips, [comb_ring, back], mixed)
    beside = swap(mixed[1], chips)
    for _ in range(4, half + 1):
        beside = ring_step(chips, [comb_ring, back], beside)
    places = jnp.concatenate([own_parts, sib_parts])
    mixed = place_columns(places, mixed[0], beside, piece)
    grad_own, grad_sib = weight_grad(
        core, [col_blocks[d] for d in dists], [comb_ring.got[d] for d in dists]
    )
    mixed, grad_own, grad_sib = ring_step(chips, [back], (mixed, grad_own, grad_sib))
    partial = (grad_own + swap(grad_sib, chips).astype(F32)).astype(BF16)
    partial, other = ring_step(chips, [back], (partial, partner(partial)))
    grad_w_out = partial.astype(F32) + other.astype(F32)
    grad_latent = back.sum().astype(BF16)
    return (mixed, grad_latent, grad_w_out)


def solution(mesh):
    rows_split = P(("dp", "expert"), None)
    experts = P("expert", None, None)
    in_specs = (rows_split, rows_split, rows_split, rows_split, P("expert", None), experts, experts)
    out_specs = (rows_split, rows_split, P("expert", None))
    return jax.shard_map(
        on_device, mesh=mesh, in_specs=in_specs, out_specs=out_specs, check_vma=False
    )
```

```python
import functools

import jax
import jax.numpy as jnp
from jax import lax
from jax.experimental import pallas as pl
from jax.experimental.pallas import tpu as pltpu
from jax.sharding import PartitionSpec as P

BF16 = jnp.bfloat16
F32 = jnp.float32
LANES = 128
NN = (((1,), (0,)), ((), ()))
NT = (((1,), (1,)), ((), ()))
TN = (((0,), (0,)), ((), ()))


def dot(a, b, dims=NN):
    return lax.dot_general(a, b, dims, preferred_element_type=F32)


def cost(flops, moved):
    return pl.CostEstimate(flops=int(flops), bytes_accessed=int(moved), transcendentals=0)


def whole(shape):
    return pl.BlockSpec(shape, lambda *_: (0,) * len(shape))


SMEM = pl.BlockSpec(memory_space=pltpu.SMEM)
ANY = pl.BlockSpec(memory_space=pl.ANY)
VMEM_BYTES = 60 * 1024 * 1024


def ring_order(chips):
    return list(range(0, chips, 2)) + list(range(1, chips, 2))[::-1]


def shift(x, chips, step):
    order = ring_order(chips)
    pairs = [
        (2 * order[j] + core, 2 * order[(j + step) % chips] + core)
        for j in range(chips)
        for core in range(2)
    ]
    return lax.ppermute(x, "expert", pairs)


def swap(x, chips):
    return lax.ppermute(x, "expert", [(i, i ^ 1) for i in range(2 * chips)])


def together(*values):
    flat, tree = jax.tree.flatten(values)
    return jax.tree.unflatten(tree, lax.optimization_barrier(flat))


class View:
    def __init__(self, x, low=0, count=None):
        self.x, self.low = x, low
        self.count = x.shape[0] - low if count is None else count

    def rows(self, start, stop):
        return View(self.x, self.low + start, stop - start)

    def value(self):
        return self.x[self.low : self.low + self.count]


def cut(views, start, stop):
    found, base = [], 0
    for v in views:
        low, high = max(start, base), min(stop, base + v.count)
        if low < high:
            found.append(v.rows(low - base, high - base))
        base += v.count
    return found


def join(views):
    values = [v.value() for v in views]
    return values[0] if len(values) == 1 else jnp.concatenate(values, axis=0)


def move_group(blocks, how):
    moved, base, found = how(join([v for b in blocks for v in b])), 0, []
    for b in blocks:
        count = sum(v.count for v in b)
        found.append([View(moved, base, count)])
        base += count
    return found


def ring_step(chips, rings, beside=()):
    sent = [r.send() for r in rings]
    up, down = join([u for u, _ in sent]), join([d for _, d in sent])
    up, down, beside = together(shift(up, chips, 1), shift(down, chips, -1), beside)
    u_base = d_base = 0
    for ring, (u, d) in zip(rings, sent):
        ring.receive(View(up, u_base, u.count), View(down, d_base, d.count))
        u_base, d_base = u_base + u.count, d_base + d.count
    return beside


class Gather:
    def __init__(self, x, chips, cut_row):
        self.half, self.steps, self.cut_row = chips // 2, 0, cut_row
        self.got, self.wire = {0: [View(x)]}, (View(x), View(x))

    def send(self):
        self.steps += 1
        up, down = self.wire
        if self.steps < self.half:
            return up, down
        return up.rows(0, self.cut_row), down.rows(self.cut_row, down.count)

    def receive(self, up, down):
        self.wire = up, down
        if self.steps < self.half:
            self.got[-self.steps], self.got[self.steps] = [up], [down]
        else:
            self.got[self.steps] = [up, down]


def total(terms):
    return functools.reduce(jnp.add, [t.astype(F32) for t in terms])


class Scatter:
    def __init__(self, parts, chips):
        self.half, self.left, self.parts, self.wire = chips // 2, chips // 2, parts, None

    def send(self):
        s, self.left = self.left, self.left - 1
        if s == self.half:
            far = total(self.parts[s]).astype(BF16)
            self.cut_row = far.shape[0] // 2
            up, down = far[: self.cut_row], far[self.cut_row :]
        else:
            (up, down), at = self.wire, self.cut_row
            a, b = total(self.parts[s]), total(self.parts[-s])
            if s == self.half - 1:
                up = jnp.concatenate([a[:at] + up.astype(F32), a[at:]], axis=0)
                down = jnp.concatenate([b[:at], b[at:] + down.astype(F32)], axis=0)
            else:
                up, down = a + up.astype(F32), b + down.astype(F32)
        return View(up.astype(BF16)), View(down.astype(BF16))

    def receive(self, up, down):
        self.wire = up.value(), down.value()

    def sum(self):
        return total(list(self.parts[0]) + list(self.wire))


def local_call(kernel, name, scalars, arrays, outs, scratch, flops, moved):
    return pl.pallas_call(
        kernel,
        in_specs=[SMEM] * len(scalars) + [ANY] * len(arrays),
        out_specs=[ANY] * len(outs),
        out_shape=outs,
        scratch_shapes=scratch,
        compiler_params=pltpu.CompilerParams(vmem_limit_bytes=VMEM_BYTES),
        cost_estimate=cost(flops, moved),
        name=name,
    )(*scalars, *arrays)


class Pieces:
    def __init__(self):
        self.arrays, self.items = [], []

    def add(self, views, slot, to=0):
        for v in views:
            known = [k for k, x in enumerate(self.arrays) if x is v.x]
            if not known:
                self.arrays.append(v.x)
                known = [len(self.arrays) - 1]
            self.items.append((known[0], v.low, v.count, slot, to))
            to += v.count

    def copies(self, refs, buffer, sems, first):
        by_slot = {}
        for i, (k, low, size, slot, to) in enumerate(self.items):
            dst = buffer.at[slot, pl.ds(to, size)]
            src = refs[k].at[pl.ds(low, size), pl.ds(0, buffer.shape[2])]
            copy = pltpu.make_async_copy(src, dst, sems.at[first + i])
            by_slot.setdefault(slot, []).append(copy)
        return by_slot


def start(copies):
    for c in copies:
        c.start()


def wait(copies):
    for c in copies:
        c.wait()


def pair_gates(gate, pair, cap, tokens):
    first = gate[2 * pair * cap : (2 * pair + 1) * cap, :]
    second = gate[(2 * pair + 1) * cap : (2 * pair + 2) * cap, :]
    empty = jnp.zeros((cap, tokens), F32)
    return jnp.concatenate(
        [jnp.concatenate([first, empty], 1), jnp.concatenate([empty, second], 1)], 0
    )


def picks(gate):
    return jnp.where(gate > 0.0, 1.0, 0.0).astype(BF16)


def tile_of(i, tile):
    return pl.ds(pl.multiple_of(i * tile, tile), tile)


def weight_copies(hbm, vmem, sems, first, tile, i):
    here, count = tile_of(i, tile), hbm[0].shape[1] // tile
    return [
        pltpu.make_async_copy(hbm[0].at[:, here], vmem[0].at[:, here], sems.at[first + i]),
        pltpu.make_async_copy(hbm[1].at[here, :], vmem[1].at[here, :], sems.at[first + count + i]),
    ]


def part_copies(both, pair, tokens, part_refs, swap_ref, sems, first):
    return [
        pltpu.make_async_copy(both.at[pair, pl.ds(0, tokens)], part_refs[pair], sems.at[first + 2 * pair]),
        pltpu.make_async_copy(
            both.at[pair, pl.ds(tokens, tokens)],
            swap_ref.at[pl.ds(pair * tokens, tokens)],
            sems.at[first + 2 * pair + 1],
        ),
    ]


def forward_kernel(pairs, cap, tokens, tile, toks, exts, me_ref, *refs):
    n_tok, n_ext = len(toks.arrays), len(exts.arrays)
    tok_refs, ext_refs = refs[:n_tok], refs[n_tok : n_tok + n_ext]
    refs = refs[n_tok + n_ext :]
    n_tok, n_ext = len(toks.items), len(exts.items)
    weights_hbm, (relu_hbm, gate_hbm) = refs[:2], refs[2:4]
    part_refs, swap_ref = refs[4 : 4 + pairs], refs[4 + pairs]
    both, ext, up, down, relu, gate, rows, acc, masks, in_sem, out_sem = refs[5 + pairs :]
    count, tiles = 2 * pairs, up.shape[1] // tile

    ext_in = exts.copies(ext_refs, ext, in_sem, 0)
    tok_in = toks.copies(tok_refs, both, in_sem, n_ext)
    for copies in (*ext_in.values(), *tok_in.values()):
        start(copies)
    first = n_ext + n_tok
    for i in range(tiles):
        start(weight_copies(weights_hbm, (up, down), in_sem, first, tile, i))

    masks[...] = jnp.zeros_like(masks)
    for b in range(count):
        wait(ext_in[b])
        extra = ext[b].astype(F32)
        mine = lax.broadcasted_iota(jnp.int32, extra.shape, 0) == me_ref[0]
        line = jnp.sum(jnp.where(mine, extra, 0.0), axis=0, keepdims=True)
        masks[b : b + 1, :] = (
            line[:, :tokens] + line[:, tokens : 2 * tokens]
        ) + line[:, 2 * tokens : 3 * tokens]
    earlier = (
        lax.broadcasted_iota(jnp.int32, (tokens, tokens), 0)
        < lax.broadcasted_iota(jnp.int32, (tokens, tokens), 1)
    )
    chosen = picks(masks[...])
    slots = dot(chosen, jnp.where(earlier, 1.0, 0.0).astype(BF16)).astype(jnp.int32)
    place = lax.broadcasted_iota(jnp.int32, (cap, tokens), 0)
    for b in range(count):
        gate[b * cap : (b + 1) * cap, :] = jnp.where(
            place == slots[b : b + 1, :], masks[b : b + 1, :], 0.0
        )
    gate_out = pltpu.make_async_copy(gate, gate_hbm, out_sem.at[0])
    gate_out.start()
    for p in range(pairs):
        wait(tok_in[p])
        pick = picks(pair_gates(gate, p, cap, tokens))
        rows[2 * p * cap : (2 * p + 2) * cap, :] = dot(pick, both[p]).astype(BF16)

    def relu_copy(i):
        here = tile_of(i, tile)
        return pltpu.make_async_copy(relu.at[:, here], relu_hbm.at[:, here], out_sem.at[1 + i])

    def hidden_tile(i, begin):
        here = tile_of(i, tile)
        wait(weight_copies(weights_hbm, (up, down), in_sem, first, tile, i))
        pre = jnp.maximum(dot(rows[...], up[:, here]), 0.0)
        relu[:, here] = pre.astype(BF16)
        relu_copy(i).start()
        out = dot((pre * pre).astype(BF16), down[here, :])
        acc[...] = out if begin else acc[...] + out

    hidden_tile(0, True)
    pl.loop(1, tiles)(lambda i: hidden_tile(i, False))

    parts_out = []
    for p in range(pairs):
        scale = pair_gates(gate, p, cap, tokens)
        result = acc[2 * p * cap : (2 * p + 2) * cap, :].astype(BF16).astype(F32)
        scaled = (result * jnp.sum(scale, axis=1, keepdims=True)).astype(BF16)
        both[p] = dot(picks(scale), scaled, TN).astype(BF16)
        out = part_copies(both, p, tokens, part_refs, swap_ref, out_sem, 1 + tiles)
        start(out)
        parts_out += out
    wait(parts_out + [gate_out] + [relu_copy(i) for i in range(tiles)])


def backward_kernel(pairs, cap, tokens, tile, toks, *refs):
    tok_refs, refs = refs[: len(toks.arrays)], refs[len(toks.arrays) :]
    relu_hbm, gate_hbm, weights_hbm = refs[0], refs[1], refs[2:4]
    part_refs, swap_ref = refs[4 : 4 + pairs], refs[4 + pairs]
    both, up, down, relu, gate, rows, acc, in_sem, out_sem = refs[5 + pairs :]
    tiles = up.shape[1] // tile

    gate_in = pltpu.make_async_copy(gate_hbm, gate, in_sem.at[0])
    gate_in.start()
    tok_in = toks.copies(tok_refs, both, in_sem, 1)
    for copies in tok_in.values():
        start(copies)
    first = 1 + len(toks.items)

    def tile_copies(i):
        here = tile_of(i, tile)
        copy = pltpu.make_async_copy(relu_hbm.at[:, here], relu.at[:, here], in_sem.at[first + i])
        return weight_copies(weights_hbm, (up, down), in_sem, first + tiles, tile, i) + [copy]

    for i in range(tiles):
        start(tile_copies(i))

    gate_in.wait()
    for p in range(pairs):
        wait(tok_in[p])
        scale = pair_gates(gate, p, cap, tokens)
        rows[2 * p * cap : (2 * p + 2) * cap, :] = (
            dot(picks(scale), both[p]) * jnp.sum(scale, axis=1, keepdims=True)
        ).astype(BF16)

    def hidden_tile(i, begin):
        here = tile_of(i, tile)
        wait(tile_copies(i))
        grad_act = dot(rows[...], down[here, :], NT)
        grad_pre = (grad_act * 2.0 * relu[:, here].astype(F32)).astype(BF16)
        out = dot(grad_pre, up[:, here], NT)
        acc[...] = out if begin else acc[...] + out

    hidden_tile(0, True)
    pl.loop(1, tiles)(lambda i: hidden_tile(i, False))

    parts_out = []
    for p in range(pairs):
        pick = picks(pair_gates(gate, p, cap, tokens))
        grad_rows = acc[2 * p * cap : (2 * p + 2) * cap, :].astype(BF16)
        both[p] = dot(pick, grad_rows, TN).astype(BF16)
        out = part_copies(both, p, tokens, part_refs, swap_ref, out_sem, 0)
        start(out)
        parts_out += out
    wait(parts_out)


def part_shapes(pairs, tokens, width):
    shapes = [jax.ShapeDtypeStruct((tokens, width), BF16)] * pairs
    return shapes + [jax.ShapeDtypeStruct((pairs * tokens, width), BF16)]


def expert_forward(me, blocks, extra, up, down, cap, tokens):
    pairs, (width, hidden) = len(blocks) // 2, up.shape
    count, tile = len(blocks), min(512, hidden)
    toks, exts = Pieces(), Pieces()
    for b, block in enumerate(blocks):
        toks.add(cut(block, 0, tokens), b // 2, b % 2 * tokens)
        exts.add(cut(block, tokens, tokens + extra), b)
    outs = [
        jax.ShapeDtypeStruct((count * cap, hidden), BF16),
        jax.ShapeDtypeStruct((count * cap, tokens), F32),
    ] + part_shapes(pairs, tokens, width)
    scratch = [
        pltpu.VMEM((pairs, 2 * tokens, width), BF16),
        pltpu.VMEM((count, extra, 3 * tokens), BF16),
        pltpu.VMEM((width, hidden), BF16),
        pltpu.VMEM((hidden, width), BF16),
        pltpu.VMEM((count * cap, hidden), BF16),
        pltpu.VMEM((count * cap, tokens), F32),
        pltpu.VMEM((count * cap, width), BF16),
        pltpu.VMEM((count * cap, width), F32),
        pltpu.VMEM((-(-count // 16) * 16, tokens), F32),
        pltpu.SemaphoreType.DMA((len(toks.items) + len(exts.items) + 2 * (hidden // tile),)),
        pltpu.SemaphoreType.DMA((1 + hidden // tile + count,)),
    ]
    out = local_call(
        functools.partial(forward_kernel, pairs, cap, tokens, tile, toks, exts),
        "expert_forward", [me], [*toks.arrays, *exts.arrays, up, down], outs, scratch,
        4 * count * cap * width * hidden, 4 * width * hidden,
    )
    return out[0], out[1], list(out[2:-1]), out[-1]


def expert_backward(blocks, relu, gate, up, down, cap, tokens):
    pairs, (width, hidden) = len(blocks) // 2, up.shape
    count, tile = len(blocks), min(512, hidden)
    toks = Pieces()
    for b, block in enumerate(blocks):
        toks.add(block, b // 2, b % 2 * tokens)
    scratch = [
        pltpu.VMEM((pairs, 2 * tokens, width), BF16),
        pltpu.VMEM((width, hidden), BF16),
        pltpu.VMEM((hidden, width), BF16),
        pltpu.VMEM((count * cap, hidden), BF16),
        pltpu.VMEM((count * cap, tokens), F32),
        pltpu.VMEM((count * cap, width), BF16),
        pltpu.VMEM((count * cap, width), F32),
        pltpu.SemaphoreType.DMA((1 + len(toks.items) + 3 * (hidden // tile),)),
        pltpu.SemaphoreType.DMA((count,)),
    ]
    out = local_call(
        functools.partial(backward_kernel, pairs, cap, tokens, tile, toks),
        "expert_backward", [], [*toks.arrays, relu, gate, up, down],
        part_shapes(pairs, tokens, width), scratch,
        4 * count * cap * width * hidden, 4 * width * hidden,
    )
    return list(out[:-1]), out[-1]


def columns(offsets, k, rows):
    return pl.ds(pl.multiple_of(offsets[k] * rows, rows), rows)


def narrow_columns(x, cols, rows):
    return x.reshape(x.shape[0], -1, rows)[:, cols, :].reshape(x.shape[0], -1)


def shard_columns(grads, offsets, k, count, rows):
    return jnp.concatenate(
        [grads[0, :, columns(offsets, k, rows)], grads[0, :, columns(offsets, count + k, rows)]], 1
    )


def stacked(mine, other):
    return jnp.concatenate([join(b) for b in (*mine, *other)], axis=0)


def projection_pieces(mine, other, rows):
    pieces = Pieces()
    for k in range(len(mine)):
        pieces.add(mine[k], k, 0)
        pieces.add(other[k], k, rows)
    return pieces


def both_cores(pair, rows):
    pieces = Pieces()
    pieces.add([View(pair[0])], 0, 0)
    pieces.add([View(pair[1])], 0, rows)
    return pieces


def grad_combined_kernel(rows, acts, weights, offsets, *refs):
    n_act, n_weight = len(acts.arrays), len(weights.arrays)
    act_refs, weight_refs = refs[:n_act], refs[n_act : n_act + n_weight]
    own_ref, sib_ref, grads, weight, out, in_sem, out_sem = refs[n_act + n_weight :]
    tokens, count = own_ref.shape[0], weight.shape[0]
    act_in = acts.copies(act_refs, grads, in_sem, 0)[0]
    weight_in = weights.copies(weight_refs, weight, in_sem, len(acts.items))
    start(act_in)
    for k in range(count):
        start(weight_in[k])
    wait(act_in)
    total = jnp.zeros(out.shape, F32)
    for k in range(count):
        wait(weight_in[k])
        total += dot(shard_columns(grads, offsets, k, count, rows), weight[k])
    out[...] = total
    copies = [
        pltpu.make_async_copy(out.at[pl.ds(0, tokens)], own_ref, out_sem.at[0]),
        pltpu.make_async_copy(out.at[pl.ds(tokens, tokens)], sib_ref, out_sem.at[1]),
    ]
    start(copies)
    wait(copies)


def grad_combined_part(offsets, grads, mine, other, rows, width):
    (tokens, features), count = grads[0].shape, len(mine)
    if rows % LANES:
        weight = stacked(mine, other)
        return [dot(narrow_columns(g, offsets, rows), weight) for g in grads]
    acts, weights = both_cores(grads, tokens), projection_pieces(mine, other, rows)
    return local_call(
        functools.partial(grad_combined_kernel, rows, acts, weights),
        "grad_combined", [offsets], [*acts.arrays, *weights.arrays],
        [jax.ShapeDtypeStruct((tokens, width), F32)] * 2,
        [
            pltpu.VMEM((1, 2 * tokens, features), BF16),
            pltpu.VMEM((count, 2 * rows, width), BF16),
            pltpu.VMEM((2 * tokens, width), F32),
            pltpu.SemaphoreType.DMA((len(acts.items) + len(weights.items),)),
            pltpu.SemaphoreType.DMA((2,)),
        ],
        8 * tokens * rows * count * width, 4 * rows * count * width,
    )


def mixed_kernel(rows, acts, weights, *refs):
    n_act, n_weight = len(acts.arrays), len(weights.arrays)
    act_refs, weight_refs = refs[:n_act], refs[n_act : n_act + n_weight]
    own_ref, sib_ref, comb, weight, out, in_sem, out_sem = refs[n_act + n_weight :]
    tokens, count = own_ref.shape[0], weight.shape[0]
    act_in = acts.copies(act_refs, comb, in_sem, 0)[0]
    weight_in = weights.copies(weight_refs, weight, in_sem, len(acts.items))
    start(act_in)
    for k in range(count):
        start(weight_in[k])
    wait(act_in)
    for k in range(count):
        wait(weight_in[k])
        block = dot(comb[0], weight[k], NT).astype(BF16)
        for part in range(2):
            here = slice((part * count + k) * rows, (part * count + k + 1) * rows)
            out[:, here] = block[:, part * rows : (part + 1) * rows]
    copies = [
        pltpu.make_async_copy(out.at[pl.ds(0, tokens)], own_ref, out_sem.at[0]),
        pltpu.make_async_copy(out.at[pl.ds(tokens, tokens)], sib_ref, out_sem.at[1]),
    ]
    start(copies)
    wait(copies)


def mixed_part(combs, mine, other, rows):
    (tokens, width), count = combs[0].shape, len(mine)
    if rows % LANES:
        weight = stacked(mine, other)
        return [dot(c, weight, NT).astype(BF16) for c in combs]
    acts, weights = both_cores(combs, tokens), projection_pieces(mine, other, rows)
    return local_call(
        functools.partial(mixed_kernel, rows, acts, weights),
        "mixed", [], [*acts.arrays, *weights.arrays],
        [jax.ShapeDtypeStruct((tokens, 2 * count * rows), BF16)] * 2,
        [
            pltpu.VMEM((1, 2 * tokens, width), BF16),
            pltpu.VMEM((count, 2 * rows, width), BF16),
            pltpu.VMEM((2 * tokens, 2 * count * rows), BF16),
            pltpu.SemaphoreType.DMA((len(acts.items) + len(weights.items),)),
            pltpu.SemaphoreType.DMA((2,)),
        ],
        8 * tokens * rows * count * width, 4 * rows * count * width,
    )


def column_blocks_kernel(chip_ref, grad_ref, *refs):
    outs, (grad, in_sem, out_sem) = refs[:-3], refs[-3:]
    fetch = pltpu.make_async_copy(grad_ref, grad, in_sem.at[0])
    fetch.start()
    fetch.wait()
    copies = []
    for k, out in enumerate(outs):
        size = out.shape[1]
        here = pl.ds(pl.multiple_of(chip_ref[k] * size, size), size)
        copies.append(pltpu.make_async_copy(grad.at[:, here], out, out_sem.at[k]))
    start(copies)
    wait(copies)


def column_blocks(chip_there, grad_out, size):
    count = chip_there.shape[0]
    return local_call(
        column_blocks_kernel, "column_blocks", [chip_there], [grad_out],
        [jax.ShapeDtypeStruct((grad_out.shape[0], size), BF16)] * count,
        [
            pltpu.VMEM(grad_out.shape, BF16),
            pltpu.SemaphoreType.DMA((1,)),
            pltpu.SemaphoreType.DMA((count,)),
        ],
        0, 4 * grad_out.size,
    )


def place_kernel(count, rows, offsets, own_ref, other_ref, out_ref):
    for k in range(count):
        block = slice(k * rows, (k + 1) * rows)
        out_ref[:, columns(offsets, k, rows)] = own_ref[:, block]
        out_ref[:, columns(offsets, count + k, rows)] = other_ref[:, block]


def place_columns(offsets, own, other, rows):
    count = offsets.shape[0] // 2
    if rows % LANES:
        back = jnp.zeros_like(offsets).at[offsets].set(jnp.arange(2 * count, dtype=offsets.dtype))
        return narrow_columns(jnp.concatenate([own, other], axis=1), back, rows)
    out = jax.ShapeDtypeStruct((own.shape[0], 2 * own.shape[1]), BF16)
    return pl.pallas_call(
        functools.partial(place_kernel, count, rows),
        in_specs=[SMEM, whole(own.shape), whole(other.shape)],
        out_specs=whole(out.shape),
        out_shape=out,
        grid=(1,),
        compiler_params=pltpu.CompilerParams(vmem_limit_bytes=VMEM_BYTES),
        cost_estimate=cost(0, 8 * own.size),
        name="place_columns",
    )(offsets, own, other)


def weight_grad_kernel(grads, combs, core_ref, *refs):
    n_grad, n_comb = len(grads.arrays), len(combs.arrays)
    grad_refs, comb_refs = refs[:n_grad], refs[n_grad : n_grad + n_comb]
    own_ref, sib_ref, grad, comb, out, rounded, in_sem, out_sem = refs[n_grad + n_comb :]
    rows = own_ref.shape[0]
    copies = grads.copies(grad_refs, grad, in_sem, 0)[0]
    copies += combs.copies(comb_refs, comb, in_sem, len(grads.items))[0]
    start(copies)
    wait(copies)
    out[...] = dot(grad[0], comb[0], TN)
    rounded[...] = out[...].astype(BF16)
    own = pl.ds(pl.multiple_of(core_ref[0] * rows, rows), rows)
    sib = pl.ds(pl.multiple_of((1 - core_ref[0]) * rows, rows), rows)
    copies = [
        pltpu.make_async_copy(out.at[own], own_ref, out_sem.at[0]),
        pltpu.make_async_copy(rounded.at[sib], sib_ref, out_sem.at[1]),
    ]
    start(copies)
    wait(copies)


def weight_grad(core, grads, combs):
    (tokens, features), width = grads[0].shape, combs[0][0].x.shape[1]
    grad, comb = Pieces(), Pieces()
    for k, (g, c) in enumerate(zip(grads, combs)):
        grad.add([View(g)], 0, k * tokens)
        comb.add(c, 0, k * tokens)
    count, rows = len(grads), features // 2
    return local_call(
        functools.partial(weight_grad_kernel, grad, comb),
        "weight_grad", [core], [*grad.arrays, *comb.arrays],
        [jax.ShapeDtypeStruct((rows, width), F32), jax.ShapeDtypeStruct((rows, width), BF16)],
        [
            pltpu.VMEM((1, count * tokens, features), BF16),
            pltpu.VMEM((1, count * tokens, width), BF16),
            pltpu.VMEM((features, width), F32),
            pltpu.VMEM((features, width), BF16),
            pltpu.SemaphoreType.DMA((len(grad.items) + len(comb.items),)),
            pltpu.SemaphoreType.DMA((2,)),
        ],
        2 * count * tokens * features * width, 2 * count * tokens * (features + width),
    )


def gate_rows(routes, gates, experts, width):
    chosen = routes.T[None] == jnp.arange(experts, dtype=jnp.int32)[:, None, None]
    gate = jnp.sum(jnp.where(chosen, gates.T[None], 0.0), axis=1)
    high = lax.reduce_precision(gate, 8, 7)
    middle = lax.reduce_precision(gate - high, 8, 7)
    low = gate - high - middle
    terms = jnp.concatenate([high, middle, low], axis=1).astype(BF16)
    return jnp.pad(terms, ((0, 0), (0, width - terms.shape[1])))


def on_device(latent, routes, gates, grad_out, w_out_t, expert_up, expert_down):
    tokens, width = latent.shape
    members = lax.axis_size("expert")
    chips = members // 2
    half = chips // 2
    capacity = max(4, tokens * routes.shape[1] * 5 // (4 * members))
    cap = -(-capacity // 16) * 16
    up_weight, down_weight = expert_up[0], expert_down[0]

    me = lax.axis_index("expert").astype(jnp.int32)
    chip, core = me // 2, me % 2
    position = jnp.where(chip % 2 == 0, chip // 2, chips - 1 - chip // 2)
    dists = [0] + [d for s in range(1, half) for d in (-s, s)] + [half]
    there = (position + jnp.array(dists, jnp.int32)) % chips
    chip_there = jnp.where(there < half, 2 * there, 2 * (chips - 1 - there) + 1)
    own_cols, sib_cols = 2 * chip_there + core, 2 * chip_there + 1 - core
    me, core = me.reshape(1), core.reshape(1)
    groups = [[0, -1, 1]] + [[-s, s] for s in range(2, half)] + [[half]]

    dp, replica = lax.axis_size("dp"), lax.axis_index("dp").astype(jnp.int32)
    shard = w_out_t.shape[0]
    piece = shard // dp
    own_parts = jnp.concatenate([own_cols * 2 + replica, own_cols * 2 + 1 - replica])
    sib_parts = jnp.concatenate([sib_cols * 2 + replica, sib_cols * 2 + 1 - replica])

    def partner(x):
        return lax.ppermute(x, "dp", [(i, (i + 1) % dp) for i in range(dp)])

    def half_rows(shard_rows, which):
        if dp == 2:
            return jnp.where(which == 0, shard_rows[:piece], shard_rows[piece:])
        return lax.dynamic_slice_in_dim(shard_rows, which * piece, piece, 0)

    def core_swap(gathered, group, size):
        own = [cut(gathered.got[d], 0, size) for d in group if d]
        other = move_group(own, lambda x: swap(x, chips))
        return [side for pair in zip(own, other) for side in pair]

    def share_out(group, parts, other, into):
        swapped = swap(other, chips)
        for i, d in enumerate(group):
            into[d] = [parts[i], swapped[i * tokens : (i + 1) * tokens]]

    extra = members
    begin, end = tokens + extra, tokens + extra + piece
    block = jnp.concatenate(
        [latent, gate_rows(routes, gates, members, width), half_rows(w_out_t, replica)], axis=0
    )
    ring = Gather(block, chips, tokens)
    forward, backward, kept = {}, {}, []

    def run_forward(i):
        pairs = core_swap(ring, groups[i], tokens + extra)
        if i == 0:
            pairs = [[View(block)], [View(block_sib)]] + pairs
        return expert_forward(me, pairs, extra, up_weight, down_weight, cap, tokens)

    def keep_forward(i, out):
        kept.append(out[:2])
        share_out(groups[i], *out[2:], forward)

    def exchange(ds):
        return partner(join([v for d in ds for v in cut(ring.got[d], begin, end)]))

    def keep_half(ds, got):
        for i, d in enumerate(ds):
            other_half[d] = got[i * piece : (i + 1) * piece]

    blocks = column_blocks(chip_there, grad_out, 2 * shard)
    grad_sib, block_sib, blocks, shard_rows = ring_step(
        chips,
        [ring],
        (swap(grad_out, chips), swap(block[: tokens + extra], chips), blocks, w_out_t),
    )
    grads = (grad_out, grad_sib)
    other_half = {0: half_rows(shard_rows, 1 - replica)}
    for s in range(2, half + 1):
        ds = [1 - s, s - 1]
        out, got = ring_step(chips, [ring], (run_forward(s - 2), exchange(ds)))
        keep_forward(s - 2, out)
        keep_half(ds, got)

    def send_columns(ds):
        return [shift(blocks[dists.index(half if d == half else -d)], chips, -d) for d in ds]

    ordered = dists[:0:-1]
    first, second = len(ordered) * 3 // 7, len(ordered) * 5 // 7
    col_blocks = {0: blocks[0]}

    out, got, cols = together(
        run_forward(half - 1), exchange([half]), send_columns(ordered[:first])
    )
    keep_forward(half - 1, out)
    keep_half([half], got)
    col_blocks.update(zip(ordered[:first], cols))

    mine = [cut(ring.got[d], begin, end) for d in dists]
    others = [[View(other_half[d])] for d in dists]
    comb = Scatter(forward, chips)
    gc_own, gc_swap = grad_combined_part(own_parts, grads, mine, others, piece, width)
    gc_other, cols = ring_step(
        chips, [comb], (swap(gc_swap, chips), send_columns(ordered[first:second]))
    )
    col_blocks.update(zip(ordered[first:second], cols))
    grad_combined = (gc_own + gc_other).astype(BF16)
    grad_ring = Gather(grad_combined, chips, tokens // 2)

    def run_backward(i):
        pairs = core_swap(grad_ring, groups[i], tokens)
        if i == 0:
            pairs = [[View(grad_combined)], [View(grad_combined_sib)]] + pairs
        return expert_backward(pairs, *kept[i], up_weight, down_weight, cap, tokens)

    grad_combined_sib = ring_step(chips, [comb, grad_ring], swap(grad_combined, chips))
    for s in range(2, half):
        out = ring_step(chips, [comb, grad_ring], run_backward(s - 2))
        share_out(groups[s - 2], *out, backward)
    combined = comb.sum().astype(BF16)
    comb_ring = Gather(combined, chips, tokens // 2)
    out = ring_step(chips, [grad_ring, comb_ring], run_backward(half - 2))
    share_out(groups[half - 2], *out, backward)
    out, cols, comb_other = ring_step(
        chips,
        [comb_ring],
        (run_backward(half - 1), send_columns(ordered[second:]), swap(combined, chips)),
    )
    share_out(groups[half - 1], *out, backward)
    col_blocks.update(zip(ordered[second:], cols))

    back = Scatter(backward, chips)
    mixed = mixed_part((combined, comb_other), mine, others, piece)
    mixed = ring_step(chips, [comb_ring, back], mixed)
    beside = swap(mixed[1], chips)
    for _ in range(4, half + 1):
        beside = ring_step(chips, [comb_ring, back], beside)
    places = jnp.concatenate([own_parts, sib_parts])
    grad_own, grad_sib = weight_grad(
        core, [col_blocks[d] for d in dists], [comb_ring.got[d] for d in dists]
    )
    grad_own, grad_sib, mixed_sib = ring_step(chips, [back], (grad_own, grad_sib, beside))
    partial = (grad_own + swap(grad_sib, chips).astype(F32)).astype(BF16)
    mixed = place_columns(places, mixed[0], mixed_sib, piece)
    partial, other, mixed = ring_step(chips, [back], (partial, partner(partial), mixed))
    grad_w_out = partial.astype(F32) + other.astype(F32)
    grad_latent = back.sum().astype(BF16)
    return (mixed, grad_latent, grad_w_out)


def solution(mesh):
    rows_split = P(("dp", "expert"), None)
    experts = P("expert", None, None)
    in_specs = (rows_split, rows_split, rows_split, rows_split, P("expert", None), experts, experts)
    out_specs = (rows_split, rows_split, P("expert", None))
    return jax.shard_map(
        on_device, mesh=mesh, in_specs=in_specs, out_specs=out_specs, check_vma=False
    )
```

```python
import functools

import jax
import jax.numpy as jnp
from jax import lax
from jax.experimental import pallas as pl
from jax.experimental.pallas import tpu as pltpu
from jax.sharding import PartitionSpec as P

BF16 = jnp.bfloat16
F32 = jnp.float32
LANES = 128
NN = (((1,), (0,)), ((), ()))
NT = (((1,), (1,)), ((), ()))
TN = (((0,), (0,)), ((), ()))


def dot(a, b, dims=NN):
    return lax.dot_general(a, b, dims, preferred_element_type=F32)


def cost(flops, moved):
    return pl.CostEstimate(flops=int(flops), bytes_accessed=int(moved), transcendentals=0)


def whole(shape):
    return pl.BlockSpec(shape, lambda *_: (0,) * len(shape))


SMEM = pl.BlockSpec(memory_space=pltpu.SMEM)
ANY = pl.BlockSpec(memory_space=pl.ANY)
VMEM_BYTES = 60 * 1024 * 1024


def ring_order(chips):
    return list(range(0, chips, 2)) + list(range(1, chips, 2))[::-1]


def shift(x, chips, step):
    order = ring_order(chips)
    pairs = [
        (2 * order[j] + core, 2 * order[(j + step) % chips] + core)
        for j in range(chips)
        for core in range(2)
    ]
    return lax.ppermute(x, "expert", pairs)


def swap(x, chips):
    return lax.ppermute(x, "expert", [(i, i ^ 1) for i in range(2 * chips)])


def together(*values):
    flat, tree = jax.tree.flatten(values)
    return jax.tree.unflatten(tree, lax.optimization_barrier(flat))


class View:
    def __init__(self, x, low=0, count=None):
        self.x, self.low = x, low
        self.count = x.shape[0] - low if count is None else count

    def rows(self, start, stop):
        return View(self.x, self.low + start, stop - start)

    def value(self):
        return self.x[self.low : self.low + self.count]


def cut(views, start, stop):
    found, base = [], 0
    for v in views:
        low, high = max(start, base), min(stop, base + v.count)
        if low < high:
            found.append(v.rows(low - base, high - base))
        base += v.count
    return found


def join(views):
    values = [v.value() for v in views]
    return values[0] if len(values) == 1 else jnp.concatenate(values, axis=0)


def move_group(blocks, how):
    moved, base, found = how(join([v for b in blocks for v in b])), 0, []
    for b in blocks:
        count = sum(v.count for v in b)
        found.append([View(moved, base, count)])
        base += count
    return found


def ring_step(chips, rings, beside=()):
    sent = [r.send() for r in rings]
    up, down = join([u for u, _ in sent]), join([d for _, d in sent])
    up, down, beside = together(shift(up, chips, 1), shift(down, chips, -1), beside)
    u_base = d_base = 0
    for ring, (u, d) in zip(rings, sent):
        ring.receive(View(up, u_base, u.count), View(down, d_base, d.count))
        u_base, d_base = u_base + u.count, d_base + d.count
    return beside


class Gather:
    def __init__(self, x, chips, cut_row):
        self.half, self.steps, self.cut_row = chips // 2, 0, cut_row
        self.got, self.wire = {0: [View(x)]}, (View(x), View(x))

    def send(self):
        self.steps += 1
        up, down = self.wire
        if self.steps < self.half:
            return up, down
        return up.rows(0, self.cut_row), down.rows(self.cut_row, down.count)

    def receive(self, up, down):
        self.wire = up, down
        if self.steps < self.half:
            self.got[-self.steps], self.got[self.steps] = [up], [down]
        else:
            self.got[self.steps] = [up, down]


def total(terms):
    return functools.reduce(jnp.add, [t.astype(F32) for t in terms])


class Scatter:
    def __init__(self, parts, chips):
        self.half, self.left, self.parts, self.wire = chips // 2, chips // 2, parts, None

    def send(self):
        s, self.left = self.left, self.left - 1
        if s == self.half:
            far = total(self.parts[s]).astype(BF16)
            self.cut_row = far.shape[0] // 2
            up, down = far[: self.cut_row], far[self.cut_row :]
        else:
            (up, down), at = self.wire, self.cut_row
            a, b = total(self.parts[s]), total(self.parts[-s])
            if s == self.half - 1:
                up = jnp.concatenate([a[:at] + up.astype(F32), a[at:]], axis=0)
                down = jnp.concatenate([b[:at], b[at:] + down.astype(F32)], axis=0)
            else:
                up, down = a + up.astype(F32), b + down.astype(F32)
        return View(up.astype(BF16)), View(down.astype(BF16))

    def receive(self, up, down):
        self.wire = up.value(), down.value()

    def sum(self):
        return total(list(self.parts[0]) + list(self.wire))


def local_call(kernel, name, scalars, arrays, outs, scratch, flops, moved):
    return pl.pallas_call(
        kernel,
        in_specs=[SMEM] * len(scalars) + [ANY] * len(arrays),
        out_specs=[ANY] * len(outs),
        out_shape=outs,
        scratch_shapes=scratch,
        compiler_params=pltpu.CompilerParams(vmem_limit_bytes=VMEM_BYTES),
        cost_estimate=cost(flops, moved),
        name=name,
    )(*scalars, *arrays)


class Pieces:
    def __init__(self):
        self.arrays, self.items = [], []

    def add(self, views, slot, to=0):
        for v in views:
            known = [k for k, x in enumerate(self.arrays) if x is v.x]
            if not known:
                self.arrays.append(v.x)
                known = [len(self.arrays) - 1]
            self.items.append((known[0], v.low, v.count, slot, to))
            to += v.count

    def copies(self, refs, buffer, sems, first):
        by_slot = {}
        for i, (k, low, size, slot, to) in enumerate(self.items):
            dst = buffer.at[slot, pl.ds(to, size)]
            src = refs[k].at[pl.ds(low, size), pl.ds(0, buffer.shape[2])]
            copy = pltpu.make_async_copy(src, dst, sems.at[first + i])
            by_slot.setdefault(slot, []).append(copy)
        return by_slot


def start(copies):
    for c in copies:
        c.start()


def wait(copies):
    for c in copies:
        c.wait()


def pair_gates(gate, pair, cap, tokens):
    first = gate[2 * pair * cap : (2 * pair + 1) * cap, :]
    second = gate[(2 * pair + 1) * cap : (2 * pair + 2) * cap, :]
    empty = jnp.zeros((cap, tokens), F32)
    return jnp.concatenate(
        [jnp.concatenate([first, empty], 1), jnp.concatenate([empty, second], 1)], 0
    )


def picks(gate):
    return jnp.where(gate > 0.0, 1.0, 0.0).astype(BF16)


def tile_of(i, tile):
    return pl.ds(pl.multiple_of(i * tile, tile), tile)


def weight_copies(hbm, vmem, sems, first, tile, i):
    here, count = tile_of(i, tile), hbm[0].shape[1] // tile
    return [
        pltpu.make_async_copy(hbm[0].at[:, here], vmem[0].at[:, here], sems.at[first + i]),
        pltpu.make_async_copy(hbm[1].at[here, :], vmem[1].at[here, :], sems.at[first + count + i]),
    ]


def part_copies(both, pair, tokens, part_refs, swap_ref, sems, first):
    return [
        pltpu.make_async_copy(both.at[pair, pl.ds(0, tokens)], part_refs[pair], sems.at[first + 2 * pair]),
        pltpu.make_async_copy(
            both.at[pair, pl.ds(tokens, tokens)],
            swap_ref.at[pl.ds(pair * tokens, tokens)],
            sems.at[first + 2 * pair + 1],
        ),
    ]


def forward_kernel(pairs, cap, tokens, tile, toks, exts, me_ref, *refs):
    n_tok, n_ext = len(toks.arrays), len(exts.arrays)
    tok_refs, ext_refs = refs[:n_tok], refs[n_tok : n_tok + n_ext]
    refs = refs[n_tok + n_ext :]
    n_tok, n_ext = len(toks.items), len(exts.items)
    weights_hbm, (relu_hbm, gate_hbm) = refs[:2], refs[2:4]
    part_refs, swap_ref = refs[4 : 4 + pairs], refs[4 + pairs]
    both, ext, up, down, relu, gate, rows, acc, masks, in_sem, out_sem = refs[5 + pairs :]
    count, tiles = 2 * pairs, up.shape[1] // tile

    ext_in = exts.copies(ext_refs, ext, in_sem, 0)
    tok_in = toks.copies(tok_refs, both, in_sem, n_ext)
    for copies in (*ext_in.values(), *tok_in.values()):
        start(copies)
    first = n_ext + n_tok
    for i in range(tiles):
        start(weight_copies(weights_hbm, (up, down), in_sem, first, tile, i))

    masks[...] = jnp.zeros_like(masks)
    for b in range(count):
        wait(ext_in[b])
        extra = ext[b].astype(F32)
        mine = lax.broadcasted_iota(jnp.int32, extra.shape, 0) == me_ref[0]
        line = jnp.sum(jnp.where(mine, extra, 0.0), axis=0, keepdims=True)
        masks[b : b + 1, :] = (
            line[:, :tokens] + line[:, tokens : 2 * tokens]
        ) + line[:, 2 * tokens : 3 * tokens]
    earlier = (
        lax.broadcasted_iota(jnp.int32, (tokens, tokens), 0)
        < lax.broadcasted_iota(jnp.int32, (tokens, tokens), 1)
    )
    chosen = picks(masks[...])
    slots = dot(chosen, jnp.where(earlier, 1.0, 0.0).astype(BF16)).astype(jnp.int32)
    place = lax.broadcasted_iota(jnp.int32, (cap, tokens), 0)
    for b in range(count):
        gate[b * cap : (b + 1) * cap, :] = jnp.where(
            place == slots[b : b + 1, :], masks[b : b + 1, :], 0.0
        )
    gate_out = pltpu.make_async_copy(gate, gate_hbm, out_sem.at[0])
    gate_out.start()
    for p in range(pairs):
        wait(tok_in[p])
        pick = picks(pair_gates(gate, p, cap, tokens))
        rows[2 * p * cap : (2 * p + 2) * cap, :] = dot(pick, both[p]).astype(BF16)

    def relu_copy(i):
        here = tile_of(i, tile)
        return pltpu.make_async_copy(relu.at[:, here], relu_hbm.at[:, here], out_sem.at[1 + i])

    def hidden_tile(i, begin):
        here = tile_of(i, tile)
        wait(weight_copies(weights_hbm, (up, down), in_sem, first, tile, i))
        pre = jnp.maximum(dot(rows[...], up[:, here]), 0.0)
        relu[:, here] = pre.astype(BF16)
        relu_copy(i).start()
        out = dot((pre * pre).astype(BF16), down[here, :])
        acc[...] = out if begin else acc[...] + out

    hidden_tile(0, True)
    pl.loop(1, tiles)(lambda i: hidden_tile(i, False))

    parts_out = []
    for p in range(pairs):
        scale = pair_gates(gate, p, cap, tokens)
        result = acc[2 * p * cap : (2 * p + 2) * cap, :].astype(BF16).astype(F32)
        scaled = (result * jnp.sum(scale, axis=1, keepdims=True)).astype(BF16)
        both[p] = dot(picks(scale), scaled, TN).astype(BF16)
        out = part_copies(both, p, tokens, part_refs, swap_ref, out_sem, 1 + tiles)
        start(out)
        parts_out += out
    wait(parts_out + [gate_out] + [relu_copy(i) for i in range(tiles)])


def backward_kernel(pairs, cap, tokens, tile, toks, *refs):
    tok_refs, refs = refs[: len(toks.arrays)], refs[len(toks.arrays) :]
    relu_hbm, gate_hbm, weights_hbm = refs[0], refs[1], refs[2:4]
    part_refs, swap_ref = refs[4 : 4 + pairs], refs[4 + pairs]
    both, up, down, relu, gate, rows, acc, in_sem, out_sem = refs[5 + pairs :]
    tiles = up.shape[1] // tile

    gate_in = pltpu.make_async_copy(gate_hbm, gate, in_sem.at[0])
    gate_in.start()
    tok_in = toks.copies(tok_refs, both, in_sem, 1)
    for copies in tok_in.values():
        start(copies)
    first = 1 + len(toks.items)

    def tile_copies(i):
        here = tile_of(i, tile)
        copy = pltpu.make_async_copy(relu_hbm.at[:, here], relu.at[:, here], in_sem.at[first + i])
        return weight_copies(weights_hbm, (up, down), in_sem, first + tiles, tile, i) + [copy]

    for i in range(tiles):
        start(tile_copies(i))

    gate_in.wait()
    for p in range(pairs):
        wait(tok_in[p])
        scale = pair_gates(gate, p, cap, tokens)
        rows[2 * p * cap : (2 * p + 2) * cap, :] = (
            dot(picks(scale), both[p]) * jnp.sum(scale, axis=1, keepdims=True)
        ).astype(BF16)

    def hidden_tile(i, begin):
        here = tile_of(i, tile)
        wait(tile_copies(i))
        grad_act = dot(rows[...], down[here, :], NT)
        grad_pre = (grad_act * 2.0 * relu[:, here].astype(F32)).astype(BF16)
        out = dot(grad_pre, up[:, here], NT)
        acc[...] = out if begin else acc[...] + out

    hidden_tile(0, True)
    pl.loop(1, tiles)(lambda i: hidden_tile(i, False))

    parts_out = []
    for p in range(pairs):
        pick = picks(pair_gates(gate, p, cap, tokens))
        grad_rows = acc[2 * p * cap : (2 * p + 2) * cap, :].astype(BF16)
        both[p] = dot(pick, grad_rows, TN).astype(BF16)
        out = part_copies(both, p, tokens, part_refs, swap_ref, out_sem, 0)
        start(out)
        parts_out += out
    wait(parts_out)


def part_shapes(pairs, tokens, width):
    shapes = [jax.ShapeDtypeStruct((tokens, width), BF16)] * pairs
    return shapes + [jax.ShapeDtypeStruct((pairs * tokens, width), BF16)]


def expert_forward(me, blocks, extra, up, down, cap, tokens):
    pairs, (width, hidden) = len(blocks) // 2, up.shape
    count, tile = len(blocks), min(512, hidden)
    toks, exts = Pieces(), Pieces()
    for b, block in enumerate(blocks):
        toks.add(cut(block, 0, tokens), b // 2, b % 2 * tokens)
        exts.add(cut(block, tokens, tokens + extra), b)
    outs = [
        jax.ShapeDtypeStruct((count * cap, hidden), BF16),
        jax.ShapeDtypeStruct((count * cap, tokens), F32),
    ] + part_shapes(pairs, tokens, width)
    scratch = [
        pltpu.VMEM((pairs, 2 * tokens, width), BF16),
        pltpu.VMEM((count, extra, 3 * tokens), BF16),
        pltpu.VMEM((width, hidden), BF16),
        pltpu.VMEM((hidden, width), BF16),
        pltpu.VMEM((count * cap, hidden), BF16),
        pltpu.VMEM((count * cap, tokens), F32),
        pltpu.VMEM((count * cap, width), BF16),
        pltpu.VMEM((count * cap, width), F32),
        pltpu.VMEM((-(-count // 16) * 16, tokens), F32),
        pltpu.SemaphoreType.DMA((len(toks.items) + len(exts.items) + 2 * (hidden // tile),)),
        pltpu.SemaphoreType.DMA((1 + hidden // tile + count,)),
    ]
    out = local_call(
        functools.partial(forward_kernel, pairs, cap, tokens, tile, toks, exts),
        "expert_forward", [me], [*toks.arrays, *exts.arrays, up, down], outs, scratch,
        4 * count * cap * width * hidden, 4 * width * hidden,
    )
    return out[0], out[1], list(out[2:-1]), out[-1]


def expert_backward(blocks, relu, gate, up, down, cap, tokens):
    pairs, (width, hidden) = len(blocks) // 2, up.shape
    count, tile = len(blocks), min(512, hidden)
    toks = Pieces()
    for b, block in enumerate(blocks):
        toks.add(block, b // 2, b % 2 * tokens)
    scratch = [
        pltpu.VMEM((pairs, 2 * tokens, width), BF16),
        pltpu.VMEM((width, hidden), BF16),
        pltpu.VMEM((hidden, width), BF16),
        pltpu.VMEM((count * cap, hidden), BF16),
        pltpu.VMEM((count * cap, tokens), F32),
        pltpu.VMEM((count * cap, width), BF16),
        pltpu.VMEM((count * cap, width), F32),
        pltpu.SemaphoreType.DMA((1 + len(toks.items) + 3 * (hidden // tile),)),
        pltpu.SemaphoreType.DMA((count,)),
    ]
    out = local_call(
        functools.partial(backward_kernel, pairs, cap, tokens, tile, toks),
        "expert_backward", [], [*toks.arrays, relu, gate, up, down],
        part_shapes(pairs, tokens, width), scratch,
        4 * count * cap * width * hidden, 4 * width * hidden,
    )
    return list(out[:-1]), out[-1]


def columns(offsets, k, rows):
    return pl.ds(pl.multiple_of(offsets[k] * rows, rows), rows)


def narrow_columns(x, cols, rows):
    return x.reshape(x.shape[0], -1, rows)[:, cols, :].reshape(x.shape[0], -1)


def shard_columns(grads, offsets, k, count, rows):
    return jnp.concatenate(
        [grads[0, :, columns(offsets, k, rows)], grads[0, :, columns(offsets, count + k, rows)]], 1
    )


def stacked(mine, other):
    return jnp.concatenate([join(b) for b in (*mine, *other)], axis=0)


def projection_pieces(mine, other, rows):
    pieces = Pieces()
    for k in range(len(mine)):
        pieces.add(mine[k], k, 0)
        pieces.add(other[k], k, rows)
    return pieces


def both_cores(pair, rows):
    pieces = Pieces()
    pieces.add([View(pair[0])], 0, 0)
    pieces.add([View(pair[1])], 0, rows)
    return pieces


def grad_combined_kernel(rows, acts, weights, offsets, *refs):
    n_act, n_weight = len(acts.arrays), len(weights.arrays)
    act_refs, weight_refs = refs[:n_act], refs[n_act : n_act + n_weight]
    own_ref, sib_ref, grads, weight, out, in_sem, out_sem = refs[n_act + n_weight :]
    tokens, count = own_ref.shape[0], weight.shape[0]
    act_in = acts.copies(act_refs, grads, in_sem, 0)[0]
    weight_in = weights.copies(weight_refs, weight, in_sem, len(acts.items))
    start(act_in)
    for k in range(count):
        start(weight_in[k])
    wait(act_in)
    total = jnp.zeros(out.shape, F32)
    for k in range(count):
        wait(weight_in[k])
        total += dot(shard_columns(grads, offsets, k, count, rows), weight[k])
    out[...] = total
    copies = [
        pltpu.make_async_copy(out.at[pl.ds(0, tokens)], own_ref, out_sem.at[0]),
        pltpu.make_async_copy(out.at[pl.ds(tokens, tokens)], sib_ref, out_sem.at[1]),
    ]
    start(copies)
    wait(copies)


def grad_combined_part(offsets, grads, mine, other, rows, width):
    (tokens, features), count = grads[0].shape, len(mine)
    if rows % LANES:
        weight = stacked(mine, other)
        return [dot(narrow_columns(g, offsets, rows), weight) for g in grads]
    acts, weights = both_cores(grads, tokens), projection_pieces(mine, other, rows)
    return local_call(
        functools.partial(grad_combined_kernel, rows, acts, weights),
        "grad_combined", [offsets], [*acts.arrays, *weights.arrays],
        [jax.ShapeDtypeStruct((tokens, width), F32)] * 2,
        [
            pltpu.VMEM((1, 2 * tokens, features), BF16),
            pltpu.VMEM((count, 2 * rows, width), BF16),
            pltpu.VMEM((2 * tokens, width), F32),
            pltpu.SemaphoreType.DMA((len(acts.items) + len(weights.items),)),
            pltpu.SemaphoreType.DMA((2,)),
        ],
        8 * tokens * rows * count * width, 4 * rows * count * width,
    )


def mixed_kernel(rows, acts, weights, *refs):
    n_act, n_weight = len(acts.arrays), len(weights.arrays)
    act_refs, weight_refs = refs[:n_act], refs[n_act : n_act + n_weight]
    own_ref, sib_ref, comb, weight, out, in_sem, out_sem = refs[n_act + n_weight :]
    tokens, count = own_ref.shape[0], weight.shape[0]
    act_in = acts.copies(act_refs, comb, in_sem, 0)[0]
    weight_in = weights.copies(weight_refs, weight, in_sem, len(acts.items))
    start(act_in)
    for k in range(count):
        start(weight_in[k])
    wait(act_in)
    for k in range(count):
        wait(weight_in[k])
        block = dot(comb[0], weight[k], NT).astype(BF16)
        for part in range(2):
            here = slice((part * count + k) * rows, (part * count + k + 1) * rows)
            out[:, here] = block[:, part * rows : (part + 1) * rows]
    copies = [
        pltpu.make_async_copy(out.at[pl.ds(0, tokens)], own_ref, out_sem.at[0]),
        pltpu.make_async_copy(out.at[pl.ds(tokens, tokens)], sib_ref, out_sem.at[1]),
    ]
    start(copies)
    wait(copies)


def mixed_part(combs, mine, other, rows):
    (tokens, width), count = combs[0].shape, len(mine)
    if rows % LANES:
        weight = stacked(mine, other)
        return [dot(c, weight, NT).astype(BF16) for c in combs]
    acts, weights = both_cores(combs, tokens), projection_pieces(mine, other, rows)
    return local_call(
        functools.partial(mixed_kernel, rows, acts, weights),
        "mixed", [], [*acts.arrays, *weights.arrays],
        [jax.ShapeDtypeStruct((tokens, 2 * count * rows), BF16)] * 2,
        [
            pltpu.VMEM((1, 2 * tokens, width), BF16),
            pltpu.VMEM((count, 2 * rows, width), BF16),
            pltpu.VMEM((2 * tokens, 2 * count * rows), BF16),
            pltpu.SemaphoreType.DMA((len(acts.items) + len(weights.items),)),
            pltpu.SemaphoreType.DMA((2,)),
        ],
        8 * tokens * rows * count * width, 4 * rows * count * width,
    )


def column_blocks_kernel(chip_ref, grad_ref, *refs):
    outs, (grad, in_sem, out_sem) = refs[:-3], refs[-3:]
    fetch = pltpu.make_async_copy(grad_ref, grad, in_sem.at[0])
    fetch.start()
    fetch.wait()
    copies = []
    for k, out in enumerate(outs):
        size = out.shape[1]
        here = pl.ds(pl.multiple_of(chip_ref[k] * size, size), size)
        copies.append(pltpu.make_async_copy(grad.at[:, here], out, out_sem.at[k]))
    start(copies)
    wait(copies)


def column_blocks(chip_there, grad_out, size):
    count = chip_there.shape[0]
    return local_call(
        column_blocks_kernel, "column_blocks", [chip_there], [grad_out],
        [jax.ShapeDtypeStruct((grad_out.shape[0], size), BF16)] * count,
        [
            pltpu.VMEM(grad_out.shape, BF16),
            pltpu.SemaphoreType.DMA((1,)),
            pltpu.SemaphoreType.DMA((count,)),
        ],
        0, 4 * grad_out.size,
    )


def place_kernel(count, rows, offsets, own_ref, other_ref, out_ref):
    for k in range(count):
        block = slice(k * rows, (k + 1) * rows)
        out_ref[:, columns(offsets, k, rows)] = own_ref[:, block]
        out_ref[:, columns(offsets, count + k, rows)] = other_ref[:, block]


def place_columns(offsets, own, other, rows):
    count = offsets.shape[0] // 2
    if rows % LANES:
        back = jnp.zeros_like(offsets).at[offsets].set(jnp.arange(2 * count, dtype=offsets.dtype))
        return narrow_columns(jnp.concatenate([own, other], axis=1), back, rows)
    out = jax.ShapeDtypeStruct((own.shape[0], 2 * own.shape[1]), BF16)
    return pl.pallas_call(
        functools.partial(place_kernel, count, rows),
        in_specs=[SMEM, whole(own.shape), whole(other.shape)],
        out_specs=whole(out.shape),
        out_shape=out,
        grid=(1,),
        compiler_params=pltpu.CompilerParams(vmem_limit_bytes=VMEM_BYTES),
        cost_estimate=cost(0, 8 * own.size),
        name="place_columns",
    )(offsets, own, other)


def weight_grad_kernel(grads, combs, core_ref, *refs):
    n_grad, n_comb = len(grads.arrays), len(combs.arrays)
    grad_refs, comb_refs = refs[:n_grad], refs[n_grad : n_grad + n_comb]
    own_ref, sib_ref, grad, comb, out, rounded, in_sem, out_sem = refs[n_grad + n_comb :]
    rows = own_ref.shape[0]
    copies = grads.copies(grad_refs, grad, in_sem, 0)[0]
    copies += combs.copies(comb_refs, comb, in_sem, len(grads.items))[0]
    start(copies)
    wait(copies)
    out[...] = dot(grad[0], comb[0], TN)
    rounded[...] = out[...].astype(BF16)
    own = pl.ds(pl.multiple_of(core_ref[0] * rows, rows), rows)
    sib = pl.ds(pl.multiple_of((1 - core_ref[0]) * rows, rows), rows)
    copies = [
        pltpu.make_async_copy(out.at[own], own_ref, out_sem.at[0]),
        pltpu.make_async_copy(rounded.at[sib], sib_ref, out_sem.at[1]),
    ]
    start(copies)
    wait(copies)


def weight_grad(core, grads, combs):
    (tokens, features), width = grads[0].shape, combs[0][0].x.shape[1]
    grad, comb = Pieces(), Pieces()
    for k, (g, c) in enumerate(zip(grads, combs)):
        grad.add([View(g)], 0, k * tokens)
        comb.add(c, 0, k * tokens)
    count, rows = len(grads), features // 2
    return local_call(
        functools.partial(weight_grad_kernel, grad, comb),
        "weight_grad", [core], [*grad.arrays, *comb.arrays],
        [jax.ShapeDtypeStruct((rows, width), F32), jax.ShapeDtypeStruct((rows, width), BF16)],
        [
            pltpu.VMEM((1, count * tokens, features), BF16),
            pltpu.VMEM((1, count * tokens, width), BF16),
            pltpu.VMEM((features, width), F32),
            pltpu.VMEM((features, width), BF16),
            pltpu.SemaphoreType.DMA((len(grad.items) + len(comb.items),)),
            pltpu.SemaphoreType.DMA((2,)),
        ],
        2 * count * tokens * features * width, 2 * count * tokens * (features + width),
    )


def gate_rows(routes, gates, experts, width):
    chosen = routes.T[None] == jnp.arange(experts, dtype=jnp.int32)[:, None, None]
    gate = jnp.sum(jnp.where(chosen, gates.T[None], 0.0), axis=1)
    high = lax.reduce_precision(gate, 8, 7)
    middle = lax.reduce_precision(gate - high, 8, 7)
    low = gate - high - middle
    terms = jnp.concatenate([high, middle, low], axis=1).astype(BF16)
    return jnp.pad(terms, ((0, 0), (0, width - terms.shape[1])))


def on_device(latent, routes, gates, grad_out, w_out_t, expert_up, expert_down):
    tokens, width = latent.shape
    members = lax.axis_size("expert")
    chips = members // 2
    half = chips // 2
    capacity = max(4, tokens * routes.shape[1] * 5 // (4 * members))
    cap = -(-capacity // 16) * 16
    up_weight, down_weight = expert_up[0], expert_down[0]

    me = lax.axis_index("expert").astype(jnp.int32)
    chip, core = me // 2, me % 2
    position = jnp.where(chip % 2 == 0, chip // 2, chips - 1 - chip // 2)
    dists = [0] + [d for s in range(1, half) for d in (-s, s)] + [half]
    there = (position + jnp.array(dists, jnp.int32)) % chips
    chip_there = jnp.where(there < half, 2 * there, 2 * (chips - 1 - there) + 1)
    own_cols, sib_cols = 2 * chip_there + core, 2 * chip_there + 1 - core
    me, core = me.reshape(1), core.reshape(1)
    groups = [[0, -1, 1]] + [[-s, s] for s in range(2, half)] + [[half]]

    dp, replica = lax.axis_size("dp"), lax.axis_index("dp").astype(jnp.int32)
    shard = w_out_t.shape[0]
    piece = shard // dp
    own_parts = jnp.concatenate([own_cols * 2 + replica, own_cols * 2 + 1 - replica])
    sib_parts = jnp.concatenate([sib_cols * 2 + replica, sib_cols * 2 + 1 - replica])

    def partner(x):
        return lax.ppermute(x, "dp", [(i, (i + 1) % dp) for i in range(dp)])

    def half_rows(shard_rows, which):
        if dp == 2:
            return jnp.where(which == 0, shard_rows[:piece], shard_rows[piece:])
        return lax.dynamic_slice_in_dim(shard_rows, which * piece, piece, 0)

    def core_swap(gathered, group, size):
        own = [cut(gathered.got[d], 0, size) for d in group if d]
        other = move_group(own, lambda x: swap(x, chips))
        return [side for pair in zip(own, other) for side in pair]

    def share_out(group, parts, other, into):
        swapped = swap(other, chips)
        for i, d in enumerate(group):
            into[d] = [parts[i], swapped[i * tokens : (i + 1) * tokens]]

    extra = members
    block = jnp.concatenate([latent, gate_rows(routes, gates, members, width)], axis=0)
    ring = Gather(block, chips, tokens // 2)
    forward, backward, kept = {}, {}, []

    def run_forward(i):
        pairs = core_swap(ring, groups[i], tokens + extra)
        if i == 0:
            pairs = [[View(block)], [View(block_sib)]] + pairs
        return expert_forward(me, pairs, extra, up_weight, down_weight, cap, tokens)

    def keep_forward(i, out):
        kept.append(out[:2])
        share_out(groups[i], *out[2:], forward)

    def exchange(ds):
        return partner(join([v for d in ds for v in proj.got[d]]))

    def keep_half(ds, got):
        for i, d in enumerate(ds):
            other_half[d] = got[i * piece : (i + 1) * piece]

    blocks = column_blocks(chip_there, grad_out, 2 * shard)
    grad_sib, block_sib, blocks, shard_rows = ring_step(
        chips,
        [ring],
        (swap(grad_out, chips), swap(block, chips), blocks, w_out_t),
    )
    grads = (grad_out, grad_sib)
    proj = Gather(half_rows(shard_rows, replica), chips, piece // 32 * 16)
    other_half = {0: half_rows(shard_rows, 1 - replica)}
    for s in range(2, half + 1):
        ds = [2 - s, s - 2] if s > 2 else []
        out, got = ring_step(
            chips, [ring, proj], (run_forward(s - 2), exchange(ds) if ds else None)
        )
        keep_forward(s - 2, out)
        keep_half(ds, got)

    def send_columns(ds):
        return [shift(blocks[dists.index(half if d == half else -d)], chips, -d) for d in ds]

    ordered = dists[:0:-1]
    first, second = len(ordered) * 3 // 7, len(ordered) * 5 // 7
    col_blocks = {0: blocks[0]}

    ds = [1 - half, half - 1]
    out, got, cols = ring_step(
        chips, [proj], (run_forward(half - 1), exchange(ds), send_columns(ordered[:first]))
    )
    keep_forward(half - 1, out)
    keep_half(ds, got)
    col_blocks.update(zip(ordered[:first], cols))
    comb = Scatter(forward, chips)
    got, cols = ring_step(
        chips, [comb], (exchange([half]), send_columns(ordered[first:second]))
    )
    keep_half([half], got)
    col_blocks.update(zip(ordered[first:second], cols))
    mine = [proj.got[d] for d in dists]
    others = [[View(other_half[d])] for d in dists]
    gc_own, gc_swap = grad_combined_part(own_parts, grads, mine, others, piece, width)
    gc_other = swap(gc_swap, chips)
    grad_combined = (gc_own + gc_other).astype(BF16)
    grad_ring = Gather(grad_combined, chips, tokens // 2)

    def run_backward(i):
        pairs = core_swap(grad_ring, groups[i], tokens)
        if i == 0:
            pairs = [[View(grad_combined)], [View(grad_combined_sib)]] + pairs
        return expert_backward(pairs, *kept[i], up_weight, down_weight, cap, tokens)

    grad_combined_sib = ring_step(chips, [comb, grad_ring], swap(grad_combined, chips))
    for s in range(2, half):
        out = ring_step(chips, [comb, grad_ring], run_backward(s - 2))
        share_out(groups[s - 2], *out, backward)
    combined = comb.sum().astype(BF16)
    comb_ring = Gather(combined, chips, tokens // 2)
    out = ring_step(chips, [grad_ring, comb_ring], run_backward(half - 2))
    share_out(groups[half - 2], *out, backward)
    out, cols, comb_other = ring_step(
        chips,
        [comb_ring],
        (run_backward(half - 1), send_columns(ordered[second:]), swap(combined, chips)),
    )
    share_out(groups[half - 1], *out, backward)
    col_blocks.update(zip(ordered[second:], cols))

    back = Scatter(backward, chips)
    mixed = mixed_part((combined, comb_other), mine, others, piece)
    mixed = ring_step(chips, [comb_ring, back], mixed)
    beside = swap(mixed[1], chips)
    for _ in range(4, half + 1):
        beside = ring_step(chips, [comb_ring, back], beside)
    places = jnp.concatenate([own_parts, sib_parts])
    grad_own, grad_sib = weight_grad(
        core, [col_blocks[d] for d in dists], [comb_ring.got[d] for d in dists]
    )
    grad_own, grad_sib, mixed_sib = ring_step(chips, [back], (grad_own, grad_sib, beside))
    partial = (grad_own + swap(grad_sib, chips).astype(F32)).astype(BF16)
    mixed = place_columns(places, mixed[0], mixed_sib, piece)
    partial, other, mixed = ring_step(chips, [back], (partial, partner(partial), mixed))
    grad_w_out = partial.astype(F32) + other.astype(F32)
    grad_latent = back.sum().astype(BF16)
    return (mixed, grad_latent, grad_w_out)


def solution(mesh):
    rows_split = P(("dp", "expert"), None)
    experts = P("expert", None, None)
    in_specs = (rows_split, rows_split, rows_split, rows_split, P("expert", None), experts, experts)
    out_specs = (rows_split, rows_split, P("expert", None))
    return jax.shard_map(
        on_device, mesh=mesh, in_specs=in_specs, out_specs=out_specs, check_vma=False
    )
```

```python
import functools

import jax
import jax.numpy as jnp
from jax import lax
from jax.experimental import pallas as pl
from jax.experimental.pallas import tpu as pltpu
from jax.sharding import PartitionSpec as P

BF16 = jnp.bfloat16
F32 = jnp.float32
LANES = 128
NN = (((1,), (0,)), ((), ()))
NT = (((1,), (1,)), ((), ()))
TN = (((0,), (0,)), ((), ()))


def dot(a, b, dims=NN):
    return lax.dot_general(a, b, dims, preferred_element_type=F32)


def cost(flops, moved):
    return pl.CostEstimate(flops=int(flops), bytes_accessed=int(moved), transcendentals=0)


def whole(shape):
    return pl.BlockSpec(shape, lambda *_: (0,) * len(shape))


SMEM = pl.BlockSpec(memory_space=pltpu.SMEM)
ANY = pl.BlockSpec(memory_space=pl.ANY)
VMEM_BYTES = 60 * 1024 * 1024


def ring_order(chips):
    return list(range(0, chips, 2)) + list(range(1, chips, 2))[::-1]


def shift(x, chips, step):
    order = ring_order(chips)
    pairs = [
        (2 * order[j] + core, 2 * order[(j + step) % chips] + core)
        for j in range(chips)
        for core in range(2)
    ]
    return lax.ppermute(x, "expert", pairs)


def swap(x, chips):
    return lax.ppermute(x, "expert", [(i, i ^ 1) for i in range(2 * chips)])


def together(*values):
    flat, tree = jax.tree.flatten(values)
    return jax.tree.unflatten(tree, lax.optimization_barrier(flat))


class View:
    def __init__(self, x, low=0, count=None):
        self.x, self.low = x, low
        self.count = x.shape[0] - low if count is None else count

    def rows(self, start, stop):
        return View(self.x, self.low + start, stop - start)

    def value(self):
        return self.x[self.low : self.low + self.count]


def cut(views, start, stop):
    found, base = [], 0
    for v in views:
        low, high = max(start, base), min(stop, base + v.count)
        if low < high:
            found.append(v.rows(low - base, high - base))
        base += v.count
    return found


def join(views):
    values = [v.value() for v in views]
    return values[0] if len(values) == 1 else jnp.concatenate(values, axis=0)


def move_group(blocks, how):
    moved, base, found = how(join([v for b in blocks for v in b])), 0, []
    for b in blocks:
        count = sum(v.count for v in b)
        found.append([View(moved, base, count)])
        base += count
    return found


def ring_step(chips, rings, beside=()):
    sent = [r.send() for r in rings]
    up, down = join([u for u, _ in sent]), join([d for _, d in sent])
    up, down, beside = together(shift(up, chips, 1), shift(down, chips, -1), beside)
    u_base = d_base = 0
    for ring, (u, d) in zip(rings, sent):
        ring.receive(View(up, u_base, u.count), View(down, d_base, d.count))
        u_base, d_base = u_base + u.count, d_base + d.count
    return beside


class Gather:
    def __init__(self, x, chips, cut_row):
        self.half, self.steps, self.cut_row = chips // 2, 0, cut_row
        self.got, self.wire = {0: [View(x)]}, (View(x), View(x))

    def send(self):
        self.steps += 1
        up, down = self.wire
        if self.steps < self.half:
            return up, down
        return up.rows(0, self.cut_row), down.rows(self.cut_row, down.count)

    def receive(self, up, down):
        self.wire = up, down
        if self.steps < self.half:
            self.got[-self.steps], self.got[self.steps] = [up], [down]
        else:
            self.got[self.steps] = [up, down]


def total(terms):
    return functools.reduce(jnp.add, [t.astype(F32) for t in terms])


class Scatter:
    def __init__(self, parts, chips):
        self.half, self.left, self.parts, self.wire = chips // 2, chips // 2, parts, None

    def send(self):
        s, self.left = self.left, self.left - 1
        if s == self.half:
            far = total(self.parts[s]).astype(BF16)
            self.cut_row = far.shape[0] // 2
            up, down = far[: self.cut_row], far[self.cut_row :]
        else:
            (up, down), at = self.wire, self.cut_row
            a, b = total(self.parts[s]), total(self.parts[-s])
            if s == self.half - 1:
                up = jnp.concatenate([a[:at] + up.astype(F32), a[at:]], axis=0)
                down = jnp.concatenate([b[:at], b[at:] + down.astype(F32)], axis=0)
            else:
                up, down = a + up.astype(F32), b + down.astype(F32)
        return View(up.astype(BF16)), View(down.astype(BF16))

    def receive(self, up, down):
        self.wire = up.value(), down.value()

    def sum(self):
        return total(list(self.parts[0]) + list(self.wire))


def local_call(kernel, name, scalars, arrays, outs, scratch, flops, moved):
    return pl.pallas_call(
        kernel,
        in_specs=[SMEM] * len(scalars) + [ANY] * len(arrays),
        out_specs=[ANY] * len(outs),
        out_shape=outs,
        scratch_shapes=scratch,
        compiler_params=pltpu.CompilerParams(vmem_limit_bytes=VMEM_BYTES),
        cost_estimate=cost(flops, moved),
        name=name,
    )(*scalars, *arrays)


class Pieces:
    def __init__(self):
        self.arrays, self.items = [], []

    def add(self, views, slot, to=0):
        for v in views:
            known = [k for k, x in enumerate(self.arrays) if x is v.x]
            if not known:
                self.arrays.append(v.x)
                known = [len(self.arrays) - 1]
            self.items.append((known[0], v.low, v.count, slot, to))
            to += v.count

    def copies(self, refs, buffer, sems, first):
        by_slot = {}
        for i, (k, low, size, slot, to) in enumerate(self.items):
            dst = buffer.at[slot, pl.ds(to, size)]
            src = refs[k].at[pl.ds(low, size), pl.ds(0, buffer.shape[2])]
            copy = pltpu.make_async_copy(src, dst, sems.at[first + i])
            by_slot.setdefault(slot, []).append(copy)
        return by_slot


def start(copies):
    for c in copies:
        c.start()


def wait(copies):
    for c in copies:
        c.wait()


def pair_gates(gate, pair, cap, tokens):
    first = gate[2 * pair * cap : (2 * pair + 1) * cap, :]
    second = gate[(2 * pair + 1) * cap : (2 * pair + 2) * cap, :]
    empty = jnp.zeros((cap, tokens), F32)
    return jnp.concatenate(
        [jnp.concatenate([first, empty], 1), jnp.concatenate([empty, second], 1)], 0
    )


def picks(gate):
    return jnp.where(gate > 0.0, 1.0, 0.0).astype(BF16)


def tile_of(i, tile):
    return pl.ds(pl.multiple_of(i * tile, tile), tile)


def weight_copies(hbm, vmem, sems, first, tile, i):
    here, count = tile_of(i, tile), hbm[0].shape[1] // tile
    return [
        pltpu.make_async_copy(hbm[0].at[:, here], vmem[0].at[:, here], sems.at[first + i]),
        pltpu.make_async_copy(hbm[1].at[here, :], vmem[1].at[here, :], sems.at[first + count + i]),
    ]


def part_copies(both, pair, tokens, part_refs, swap_ref, sems, first):
    return [
        pltpu.make_async_copy(both.at[pair, pl.ds(0, tokens)], part_refs[pair], sems.at[first + 2 * pair]),
        pltpu.make_async_copy(
            both.at[pair, pl.ds(tokens, tokens)],
            swap_ref.at[pl.ds(pair * tokens, tokens)],
            sems.at[first + 2 * pair + 1],
        ),
    ]


def forward_kernel(pairs, cap, tokens, tile, toks, exts, me_ref, *refs):
    n_tok, n_ext = len(toks.arrays), len(exts.arrays)
    tok_refs, ext_refs = refs[:n_tok], refs[n_tok : n_tok + n_ext]
    refs = refs[n_tok + n_ext :]
    n_tok, n_ext = len(toks.items), len(exts.items)
    weights_hbm, (relu_hbm, gate_hbm) = refs[:2], refs[2:4]
    part_refs, swap_ref = refs[4 : 4 + pairs], refs[4 + pairs]
    both, ext, up, down, relu, gate, rows, acc, masks, in_sem, out_sem = refs[5 + pairs :]
    count, tiles = 2 * pairs, up.shape[1] // tile

    ext_in = exts.copies(ext_refs, ext, in_sem, 0)
    tok_in = toks.copies(tok_refs, both, in_sem, n_ext)
    for copies in (*ext_in.values(), *tok_in.values()):
        start(copies)
    first = n_ext + n_tok
    for i in range(tiles):
        start(weight_copies(weights_hbm, (up, down), in_sem, first, tile, i))

    masks[...] = jnp.zeros_like(masks)
    for b in range(count):
        wait(ext_in[b])
        extra = ext[b].astype(F32)
        mine = lax.broadcasted_iota(jnp.int32, extra.shape, 0) == me_ref[0]
        line = jnp.sum(jnp.where(mine, extra, 0.0), axis=0, keepdims=True)
        masks[b : b + 1, :] = (
            line[:, :tokens] + line[:, tokens : 2 * tokens]
        ) + line[:, 2 * tokens : 3 * tokens]
    earlier = (
        lax.broadcasted_iota(jnp.int32, (tokens, tokens), 0)
        < lax.broadcasted_iota(jnp.int32, (tokens, tokens), 1)
    )
    chosen = picks(masks[...])
    slots = dot(chosen, jnp.where(earlier, 1.0, 0.0).astype(BF16)).astype(jnp.int32)
    place = lax.broadcasted_iota(jnp.int32, (cap, tokens), 0)
    for b in range(count):
        gate[b * cap : (b + 1) * cap, :] = jnp.where(
            place == slots[b : b + 1, :], masks[b : b + 1, :], 0.0
        )
    gate_out = pltpu.make_async_copy(gate, gate_hbm, out_sem.at[0])
    gate_out.start()
    for p in range(pairs):
        wait(tok_in[p])
        pick = picks(pair_gates(gate, p, cap, tokens))
        rows[2 * p * cap : (2 * p + 2) * cap, :] = dot(pick, both[p]).astype(BF16)

    def relu_copy(i):
        here = tile_of(i, tile)
        return pltpu.make_async_copy(relu.at[:, here], relu_hbm.at[:, here], out_sem.at[1 + i])

    def hidden_tile(i, begin):
        here = tile_of(i, tile)
        wait(weight_copies(weights_hbm, (up, down), in_sem, first, tile, i))
        pre = jnp.maximum(dot(rows[...], up[:, here]), 0.0)
        relu[:, here] = pre.astype(BF16)
        relu_copy(i).start()
        out = dot((pre * pre).astype(BF16), down[here, :])
        acc[...] = out if begin else acc[...] + out

    hidden_tile(0, True)
    pl.loop(1, tiles)(lambda i: hidden_tile(i, False))

    parts_out = []
    for p in range(pairs):
        scale = pair_gates(gate, p, cap, tokens)
        result = acc[2 * p * cap : (2 * p + 2) * cap, :].astype(BF16).astype(F32)
        scaled = (result * jnp.sum(scale, axis=1, keepdims=True)).astype(BF16)
        both[p] = dot(picks(scale), scaled, TN).astype(BF16)
        out = part_copies(both, p, tokens, part_refs, swap_ref, out_sem, 1 + tiles)
        start(out)
        parts_out += out
    wait(parts_out + [gate_out] + [relu_copy(i) for i in range(tiles)])


def backward_kernel(pairs, cap, tokens, tile, toks, *refs):
    tok_refs, refs = refs[: len(toks.arrays)], refs[len(toks.arrays) :]
    relu_hbm, gate_hbm, weights_hbm = refs[0], refs[1], refs[2:4]
    part_refs, swap_ref = refs[4 : 4 + pairs], refs[4 + pairs]
    both, up, down, relu, gate, rows, acc, in_sem, out_sem = refs[5 + pairs :]
    tiles = up.shape[1] // tile

    gate_in = pltpu.make_async_copy(gate_hbm, gate, in_sem.at[0])
    gate_in.start()
    tok_in = toks.copies(tok_refs, both, in_sem, 1)
    for copies in tok_in.values():
        start(copies)
    first = 1 + len(toks.items)

    def tile_copies(i):
        here = tile_of(i, tile)
        copy = pltpu.make_async_copy(relu_hbm.at[:, here], relu.at[:, here], in_sem.at[first + i])
        return weight_copies(weights_hbm, (up, down), in_sem, first + tiles, tile, i) + [copy]

    for i in range(tiles):
        start(tile_copies(i))

    gate_in.wait()
    for p in range(pairs):
        wait(tok_in[p])
        scale = pair_gates(gate, p, cap, tokens)
        rows[2 * p * cap : (2 * p + 2) * cap, :] = (
            dot(picks(scale), both[p]) * jnp.sum(scale, axis=1, keepdims=True)
        ).astype(BF16)

    def hidden_tile(i, begin):
        here = tile_of(i, tile)
        wait(tile_copies(i))
        grad_act = dot(rows[...], down[here, :], NT)
        grad_pre = (grad_act * 2.0 * relu[:, here].astype(F32)).astype(BF16)
        out = dot(grad_pre, up[:, here], NT)
        acc[...] = out if begin else acc[...] + out

    hidden_tile(0, True)
    pl.loop(1, tiles)(lambda i: hidden_tile(i, False))

    parts_out = []
    for p in range(pairs):
        pick = picks(pair_gates(gate, p, cap, tokens))
        grad_rows = acc[2 * p * cap : (2 * p + 2) * cap, :].astype(BF16)
        both[p] = dot(pick, grad_rows, TN).astype(BF16)
        out = part_copies(both, p, tokens, part_refs, swap_ref, out_sem, 0)
        start(out)
        parts_out += out
    wait(parts_out)


def part_shapes(pairs, tokens, width):
    shapes = [jax.ShapeDtypeStruct((tokens, width), BF16)] * pairs
    return shapes + [jax.ShapeDtypeStruct((pairs * tokens, width), BF16)]


def expert_forward(me, blocks, extra, up, down, cap, tokens):
    pairs, (width, hidden) = len(blocks) // 2, up.shape
    count, tile = len(blocks), min(512, hidden)
    toks, exts = Pieces(), Pieces()
    for b, block in enumerate(blocks):
        toks.add(cut(block, 0, tokens), b // 2, b % 2 * tokens)
        exts.add(cut(block, tokens, tokens + extra), b)
    outs = [
        jax.ShapeDtypeStruct((count * cap, hidden), BF16),
        jax.ShapeDtypeStruct((count * cap, tokens), F32),
    ] + part_shapes(pairs, tokens, width)
    scratch = [
        pltpu.VMEM((pairs, 2 * tokens, width), BF16),
        pltpu.VMEM((count, extra, 3 * tokens), BF16),
        pltpu.VMEM((width, hidden), BF16),
        pltpu.VMEM((hidden, width), BF16),
        pltpu.VMEM((count * cap, hidden), BF16),
        pltpu.VMEM((count * cap, tokens), F32),
        pltpu.VMEM((count * cap, width), BF16),
        pltpu.VMEM((count * cap, width), F32),
        pltpu.VMEM((-(-count // 16) * 16, tokens), F32),
        pltpu.SemaphoreType.DMA((len(toks.items) + len(exts.items) + 2 * (hidden // tile),)),
        pltpu.SemaphoreType.DMA((1 + hidden // tile + count,)),
    ]
    out = local_call(
        functools.partial(forward_kernel, pairs, cap, tokens, tile, toks, exts),
        "expert_forward", [me], [*toks.arrays, *exts.arrays, up, down], outs, scratch,
        4 * count * cap * width * hidden, 4 * width * hidden,
    )
    return out[0], out[1], list(out[2:-1]), out[-1]


def expert_backward(blocks, relu, gate, up, down, cap, tokens):
    pairs, (width, hidden) = len(blocks) // 2, up.shape
    count, tile = len(blocks), min(512, hidden)
    toks = Pieces()
    for b, block in enumerate(blocks):
        toks.add(block, b // 2, b % 2 * tokens)
    scratch = [
        pltpu.VMEM((pairs, 2 * tokens, width), BF16),
        pltpu.VMEM((width, hidden), BF16),
        pltpu.VMEM((hidden, width), BF16),
        pltpu.VMEM((count * cap, hidden), BF16),
        pltpu.VMEM((count * cap, tokens), F32),
        pltpu.VMEM((count * cap, width), BF16),
        pltpu.VMEM((count * cap, width), F32),
        pltpu.SemaphoreType.DMA((1 + len(toks.items) + 3 * (hidden // tile),)),
        pltpu.SemaphoreType.DMA((count,)),
    ]
    out = local_call(
        functools.partial(backward_kernel, pairs, cap, tokens, tile, toks),
        "expert_backward", [], [*toks.arrays, relu, gate, up, down],
        part_shapes(pairs, tokens, width), scratch,
        4 * count * cap * width * hidden, 4 * width * hidden,
    )
    return list(out[:-1]), out[-1]


def columns(offsets, k, rows):
    return pl.ds(pl.multiple_of(offsets[k] * rows, rows), rows)


def narrow_columns(x, cols, rows):
    return x.reshape(x.shape[0], -1, rows)[:, cols, :].reshape(x.shape[0], -1)


def shard_columns(grads, offsets, k, count, rows):
    return jnp.concatenate(
        [grads[0, :, columns(offsets, k, rows)], grads[0, :, columns(offsets, count + k, rows)]], 1
    )


def stacked(mine, other):
    return jnp.concatenate([join(b) for b in (*mine, *other)], axis=0)


def projection_pieces(mine, other, rows):
    pieces = Pieces()
    for k in range(len(mine)):
        pieces.add(mine[k], k, 0)
        pieces.add(other[k], k, rows)
    return pieces


def both_cores(pair, rows):
    pieces = Pieces()
    pieces.add([View(pair[0])], 0, 0)
    pieces.add([View(pair[1])], 0, rows)
    return pieces


def grad_combined_kernel(rows, acts, weights, offsets, *refs):
    n_act, n_weight = len(acts.arrays), len(weights.arrays)
    act_refs, weight_refs = refs[:n_act], refs[n_act : n_act + n_weight]
    own_ref, sib_ref, grads, weight, out, in_sem, out_sem = refs[n_act + n_weight :]
    tokens, count = own_ref.shape[0], weight.shape[0]
    act_in = acts.copies(act_refs, grads, in_sem, 0)[0]
    weight_in = weights.copies(weight_refs, weight, in_sem, len(acts.items))
    start(act_in)
    for k in range(count):
        start(weight_in[k])
    wait(act_in)
    total = jnp.zeros(out.shape, F32)
    for k in range(count):
        wait(weight_in[k])
        total += dot(shard_columns(grads, offsets, k, count, rows), weight[k])
    out[...] = total
    copies = [
        pltpu.make_async_copy(out.at[pl.ds(0, tokens)], own_ref, out_sem.at[0]),
        pltpu.make_async_copy(out.at[pl.ds(tokens, tokens)], sib_ref, out_sem.at[1]),
    ]
    start(copies)
    wait(copies)


def grad_combined_part(offsets, grads, mine, other, rows, width):
    (tokens, features), count = grads[0].shape, len(mine)
    if rows % LANES:
        weight = stacked(mine, other)
        return [dot(narrow_columns(g, offsets, rows), weight) for g in grads]
    acts, weights = both_cores(grads, tokens), projection_pieces(mine, other, rows)
    return local_call(
        functools.partial(grad_combined_kernel, rows, acts, weights),
        "grad_combined", [offsets], [*acts.arrays, *weights.arrays],
        [jax.ShapeDtypeStruct((tokens, width), F32)] * 2,
        [
            pltpu.VMEM((1, 2 * tokens, features), BF16),
            pltpu.VMEM((count, 2 * rows, width), BF16),
            pltpu.VMEM((2 * tokens, width), F32),
            pltpu.SemaphoreType.DMA((len(acts.items) + len(weights.items),)),
            pltpu.SemaphoreType.DMA((2,)),
        ],
        8 * tokens * rows * count * width, 4 * rows * count * width,
    )


def mixed_kernel(rows, acts, weights, *refs):
    n_act, n_weight = len(acts.arrays), len(weights.arrays)
    act_refs, weight_refs = refs[:n_act], refs[n_act : n_act + n_weight]
    own_ref, sib_ref, comb, weight, out, in_sem, out_sem = refs[n_act + n_weight :]
    tokens, count = own_ref.shape[0], weight.shape[0]
    act_in = acts.copies(act_refs, comb, in_sem, 0)[0]
    weight_in = weights.copies(weight_refs, weight, in_sem, len(acts.items))
    start(act_in)
    for k in range(count):
        start(weight_in[k])
    wait(act_in)
    for k in range(count):
        wait(weight_in[k])
        block = dot(comb[0], weight[k], NT).astype(BF16)
        for part in range(2):
            here = slice((part * count + k) * rows, (part * count + k + 1) * rows)
            out[:, here] = block[:, part * rows : (part + 1) * rows]
    copies = [
        pltpu.make_async_copy(out.at[pl.ds(0, tokens)], own_ref, out_sem.at[0]),
        pltpu.make_async_copy(out.at[pl.ds(tokens, tokens)], sib_ref, out_sem.at[1]),
    ]
    start(copies)
    wait(copies)


def mixed_part(combs, mine, other, rows):
    (tokens, width), count = combs[0].shape, len(mine)
    if rows % LANES:
        weight = stacked(mine, other)
        return [dot(c, weight, NT).astype(BF16) for c in combs]
    acts, weights = both_cores(combs, tokens), projection_pieces(mine, other, rows)
    return local_call(
        functools.partial(mixed_kernel, rows, acts, weights),
        "mixed", [], [*acts.arrays, *weights.arrays],
        [jax.ShapeDtypeStruct((tokens, 2 * count * rows), BF16)] * 2,
        [
            pltpu.VMEM((1, 2 * tokens, width), BF16),
            pltpu.VMEM((count, 2 * rows, width), BF16),
            pltpu.VMEM((2 * tokens, 2 * count * rows), BF16),
            pltpu.SemaphoreType.DMA((len(acts.items) + len(weights.items),)),
            pltpu.SemaphoreType.DMA((2,)),
        ],
        8 * tokens * rows * count * width, 4 * rows * count * width,
    )


def column_blocks_kernel(chip_ref, grad_ref, *refs):
    outs, (grad, in_sem, out_sem) = refs[:-3], refs[-3:]
    fetch = pltpu.make_async_copy(grad_ref, grad, in_sem.at[0])
    fetch.start()
    fetch.wait()
    copies = []
    for k, out in enumerate(outs):
        size = out.shape[1]
        here = pl.ds(pl.multiple_of(chip_ref[k] * size, size), size)
        copies.append(pltpu.make_async_copy(grad.at[:, here], out, out_sem.at[k]))
    start(copies)
    wait(copies)


def column_blocks(chip_there, grad_out, size):
    count = chip_there.shape[0]
    return local_call(
        column_blocks_kernel, "column_blocks", [chip_there], [grad_out],
        [jax.ShapeDtypeStruct((grad_out.shape[0], size), BF16)] * count,
        [
            pltpu.VMEM(grad_out.shape, BF16),
            pltpu.SemaphoreType.DMA((1,)),
            pltpu.SemaphoreType.DMA((count,)),
        ],
        0, 4 * grad_out.size,
    )


def place_kernel(count, rows, offsets, own_ref, other_ref, out_ref):
    for k in range(count):
        block = slice(k * rows, (k + 1) * rows)
        out_ref[:, columns(offsets, k, rows)] = own_ref[:, block]
        out_ref[:, columns(offsets, count + k, rows)] = other_ref[:, block]


def place_columns(offsets, own, other, rows):
    count = offsets.shape[0] // 2
    if rows % LANES:
        back = jnp.zeros_like(offsets).at[offsets].set(jnp.arange(2 * count, dtype=offsets.dtype))
        return narrow_columns(jnp.concatenate([own, other], axis=1), back, rows)
    out = jax.ShapeDtypeStruct((own.shape[0], 2 * own.shape[1]), BF16)
    return pl.pallas_call(
        functools.partial(place_kernel, count, rows),
        in_specs=[SMEM, whole(own.shape), whole(other.shape)],
        out_specs=whole(out.shape),
        out_shape=out,
        grid=(1,),
        compiler_params=pltpu.CompilerParams(vmem_limit_bytes=VMEM_BYTES),
        cost_estimate=cost(0, 8 * own.size),
        name="place_columns",
    )(offsets, own, other)


def weight_grad_kernel(grads, combs, core_ref, *refs):
    n_grad, n_comb = len(grads.arrays), len(combs.arrays)
    grad_refs, comb_refs = refs[:n_grad], refs[n_grad : n_grad + n_comb]
    own_ref, sib_ref, grad, comb, out, rounded, in_sem, out_sem = refs[n_grad + n_comb :]
    rows = own_ref.shape[0]
    copies = grads.copies(grad_refs, grad, in_sem, 0)[0]
    copies += combs.copies(comb_refs, comb, in_sem, len(grads.items))[0]
    start(copies)
    wait(copies)
    out[...] = dot(grad[0], comb[0], TN)
    rounded[...] = out[...].astype(BF16)
    own = pl.ds(pl.multiple_of(core_ref[0] * rows, rows), rows)
    sib = pl.ds(pl.multiple_of((1 - core_ref[0]) * rows, rows), rows)
    copies = [
        pltpu.make_async_copy(out.at[own], own_ref, out_sem.at[0]),
        pltpu.make_async_copy(rounded.at[sib], sib_ref, out_sem.at[1]),
    ]
    start(copies)
    wait(copies)


def weight_grad(core, grads, combs):
    (tokens, features), width = grads[0].shape, combs[0][0].x.shape[1]
    grad, comb = Pieces(), Pieces()
    for k, (g, c) in enumerate(zip(grads, combs)):
        grad.add([View(g)], 0, k * tokens)
        comb.add(c, 0, k * tokens)
    count, rows = len(grads), features // 2
    return local_call(
        functools.partial(weight_grad_kernel, grad, comb),
        "weight_grad", [core], [*grad.arrays, *comb.arrays],
        [jax.ShapeDtypeStruct((rows, width), F32), jax.ShapeDtypeStruct((rows, width), BF16)],
        [
            pltpu.VMEM((1, count * tokens, features), BF16),
            pltpu.VMEM((1, count * tokens, width), BF16),
            pltpu.VMEM((features, width), F32),
            pltpu.VMEM((features, width), BF16),
            pltpu.SemaphoreType.DMA((len(grad.items) + len(comb.items),)),
            pltpu.SemaphoreType.DMA((2,)),
        ],
        2 * count * tokens * features * width, 2 * count * tokens * (features + width),
    )


def gate_rows(routes, gates, experts, width):
    chosen = routes.T[None] == jnp.arange(experts, dtype=jnp.int32)[:, None, None]
    gate = jnp.sum(jnp.where(chosen, gates.T[None], 0.0), axis=1)
    high = lax.reduce_precision(gate, 8, 7)
    middle = lax.reduce_precision(gate - high, 8, 7)
    low = gate - high - middle
    terms = jnp.concatenate([high, middle, low], axis=1).astype(BF16)
    return jnp.pad(terms, ((0, 0), (0, width - terms.shape[1])))


def on_device(latent, routes, gates, grad_out, w_out_t, expert_up, expert_down):
    tokens, width = latent.shape
    members = lax.axis_size("expert")
    chips = members // 2
    half = chips // 2
    capacity = max(4, tokens * routes.shape[1] * 5 // (4 * members))
    cap = -(-capacity // 16) * 16
    up_weight, down_weight = expert_up[0], expert_down[0]

    me = lax.axis_index("expert").astype(jnp.int32)
    chip, core = me // 2, me % 2
    position = jnp.where(chip % 2 == 0, chip // 2, chips - 1 - chip // 2)
    dists = [0] + [d for s in range(1, half) for d in (-s, s)] + [half]
    there = (position + jnp.array(dists, jnp.int32)) % chips
    chip_there = jnp.where(there < half, 2 * there, 2 * (chips - 1 - there) + 1)
    own_cols, sib_cols = 2 * chip_there + core, 2 * chip_there + 1 - core
    me, core = me.reshape(1), core.reshape(1)
    groups = [[0, -1, 1]] + [[-s, s] for s in range(2, half)] + [[half]]

    dp, replica = lax.axis_size("dp"), lax.axis_index("dp").astype(jnp.int32)
    shard = w_out_t.shape[0]
    piece = shard // dp
    own_parts = jnp.concatenate([own_cols * 2 + replica, own_cols * 2 + 1 - replica])
    sib_parts = jnp.concatenate([sib_cols * 2 + replica, sib_cols * 2 + 1 - replica])

    def partner(x):
        return lax.ppermute(x, "dp", [(i, (i + 1) % dp) for i in range(dp)])

    def half_rows(shard_rows, which):
        if dp == 2:
            return jnp.where(which == 0, shard_rows[:piece], shard_rows[piece:])
        return lax.dynamic_slice_in_dim(shard_rows, which * piece, piece, 0)

    def core_swap(gathered, group, size):
        own = [cut(gathered.got[d], 0, size) for d in group if d]
        other = move_group(own, lambda x: swap(x, chips))
        return [side for pair in zip(own, other) for side in pair]

    def share_out(group, parts, other, into):
        swapped = swap(other, chips)
        for i, d in enumerate(group):
            into[d] = [parts[i], swapped[i * tokens : (i + 1) * tokens]]

    extra = members
    block = jnp.concatenate([latent, gate_rows(routes, gates, members, width)], axis=0)
    ring = Gather(block, chips, tokens // 2)
    forward, backward, kept = {}, {}, []

    def run_forward(i):
        pairs = core_swap(ring, groups[i], tokens + extra)
        if i == 0:
            pairs = [[View(block)], [View(block_sib)]] + pairs
        return expert_forward(me, pairs, extra, up_weight, down_weight, cap, tokens)

    def keep_forward(i, out):
        kept.append(out[:2])
        share_out(groups[i], *out[2:], forward)

    def exchange(ds):
        return partner(join([v for d in ds for v in proj.got[d]]))

    def keep_half(ds, got):
        for i, d in enumerate(ds):
            other_half[d] = got[i * piece : (i + 1) * piece]

    blocks = column_blocks(chip_there, grad_out, 2 * shard)
    half_mine, half_other = half_rows(w_out_t, replica), half_rows(w_out_t, 1 - replica)
    grad_sib, block_sib, blocks, half_mine, half_other = ring_step(
        chips,
        [ring],
        (swap(grad_out, chips), swap(block, chips), blocks, half_mine, half_other),
    )
    grads = (grad_out, grad_sib)
    proj = Gather(half_mine, chips, piece // 32 * 16)
    other_half = {0: half_other}
    for s in range(2, half + 1):
        ds = [2 - s, s - 2] if s > 2 else []
        out, got = ring_step(
            chips, [ring, proj], (run_forward(s - 2), exchange(ds) if ds else None)
        )
        keep_forward(s - 2, out)
        keep_half(ds, got)

    def send_columns(ds):
        return [shift(blocks[dists.index(half if d == half else -d)], chips, -d) for d in ds]

    ordered = dists[:0:-1]
    first, second = len(ordered) * 3 // 7, len(ordered) * 5 // 7
    col_blocks = {0: blocks[0]}

    ds = [1 - half, half - 1]
    out, got, cols = ring_step(
        chips, [proj], (run_forward(half - 1), exchange(ds), send_columns(ordered[:first]))
    )
    keep_forward(half - 1, out)
    keep_half(ds, got)
    col_blocks.update(zip(ordered[:first], cols))
    comb = Scatter(forward, chips)
    got, cols = ring_step(
        chips, [comb], (exchange([half]), send_columns(ordered[first:second]))
    )
    keep_half([half], got)
    col_blocks.update(zip(ordered[first:second], cols))
    mine = [proj.got[d] for d in dists]
    others = [[View(other_half[d])] for d in dists]
    gc_own, gc_swap = grad_combined_part(own_parts, grads, mine, others, piece, width)
    gc_other = swap(gc_swap, chips)
    grad_combined = (gc_own + gc_other).astype(BF16)
    grad_ring = Gather(grad_combined, chips, tokens // 2)

    def run_backward(i):
        pairs = core_swap(grad_ring, groups[i], tokens)
        if i == 0:
            pairs = [[View(grad_combined)], [View(grad_combined_sib)]] + pairs
        return expert_backward(pairs, *kept[i], up_weight, down_weight, cap, tokens)

    grad_combined_sib = ring_step(chips, [comb, grad_ring], swap(grad_combined, chips))
    for s in range(2, half):
        out = ring_step(chips, [comb, grad_ring], run_backward(s - 2))
        share_out(groups[s - 2], *out, backward)
    combined = comb.sum().astype(BF16)
    comb_ring = Gather(combined, chips, tokens // 2)
    out = ring_step(chips, [grad_ring, comb_ring], run_backward(half - 2))
    share_out(groups[half - 2], *out, backward)
    out, cols, comb_other = ring_step(
        chips,
        [comb_ring],
        (run_backward(half - 1), send_columns(ordered[second:]), swap(combined, chips)),
    )
    share_out(groups[half - 1], *out, backward)
    col_blocks.update(zip(ordered[second:], cols))

    back = Scatter(backward, chips)
    mixed = mixed_part((combined, comb_other), mine, others, piece)
    mixed = ring_step(chips, [comb_ring, back], mixed)
    beside = swap(mixed[1], chips)
    for _ in range(4, half + 1):
        beside = ring_step(chips, [comb_ring, back], beside)
    places = jnp.concatenate([own_parts, sib_parts])
    grad_own, grad_sib = weight_grad(
        core, [col_blocks[d] for d in dists], [comb_ring.got[d] for d in dists]
    )
    grad_own, grad_sib, mixed_sib = ring_step(chips, [back], (grad_own, grad_sib, beside))
    partial = (grad_own + swap(grad_sib, chips).astype(F32)).astype(BF16)
    mixed = place_columns(places, mixed[0], mixed_sib, piece)
    partial, other, mixed = ring_step(chips, [back], (partial, partner(partial), mixed))
    grad_w_out = partial.astype(F32) + other.astype(F32)
    grad_latent = back.sum().astype(BF16)
    return (mixed, grad_latent, grad_w_out)


def solution(mesh):
    rows_split = P(("dp", "expert"), None)
    experts = P("expert", None, None)
    in_specs = (rows_split, rows_split, rows_split, rows_split, P("expert", None), experts, experts)
    out_specs = (rows_split, rows_split, P("expert", None))
    return jax.shard_map(
        on_device, mesh=mesh, in_specs=in_specs, out_specs=out_specs, check_vma=False
    )
```
